256 devices in a mesh: win: 32 (over x, z), head: 8 (over y, core).
Axes of the slice: x: 4, y: 4, z: 8, core: 2. Of those that a mesh axis runs over, the one named last changes fastest.
Arguments:
- latents: bfloat16 [16384, 3072], P(('win', 'head'))
- modulation: float32 [3, 3072], replicated, may hold values from -2.5 to 2.5
- qkv_weight: bfloat16 [3072, 3, 3072], P(None, None, 'head'), may hold values from -0.109375 to 0.109375
- qkv_bias: float32 [3, 3072], P(None, 'head'), may hold values from -3 to 3
- norm_gain: float32 [2, 128], replicated, may hold values from 1 to 2.5
- out_weight: bfloat16 [3072, 3072], P('head'), may hold values from -0.109375 to 0.109375
- out_bias: float32 [3072], replicated, may hold values from -3 to 3
- key_tiles: int32 [32, 16], P('win'), may hold values from 0 to 127, as said below
- key_count: int32 [32], P('win'), may hold values from 8 to 16, as said below
- strip_rows: int32 [32], replicated, may hold values from 16 to 64, as said below
Outputs:
- blended_out: bfloat16 [16384, 3072], P(('win', 'head'))
The draws below stay inside these ranges and needn't reach their ends.
Inputs may be any that keep to these rules, and one draw needn't show every extreme that they name: `key_tiles`: entries 2 * j to 2 * j + 1 of window w's row are distinct tiles of window (w + o) mod 32, with o = j // 2 + 1 for even j and o = -(j // 2 + 1) for odd j. `key_count`: some window reads all 16 entries. `strip_rows`: some pair of windows shares 64 rows.
All inputs are finite; a program needn't handle non-finite values.
Results may differ from the reference program's by a relative error of at most 0.0028.
Values may be sent and summed in bfloat16 or wider, within the bound.
No kernel may reach another device: no remote copies, remote signals or barrier semaphores. Data moves between devices by JAX's collectives and lax.ppermute only.
A program may use at most 128 MiB of HBM per device.

```python
import math
import jax
import jax.numpy as jnp
from jax import lax

HEADS = 24
HEAD_DIM = 128
TILE = 128
TW = 4
NB = 8
CAP = 2
OV = 64
D = 3072
WINDOWS = 32
TOKENS = 16384


def draw_latents(key, part):
    key_base = jax.random.fold_in(key, 11)
    key_rows = jax.random.fold_in(key_base, 1)
    key_cols = jax.random.fold_in(key_base, 2)
    key_main = jax.random.fold_in(key_base, 3)
    row_scale = jnp.exp(jax.random.uniform(key_rows, (TOKENS, 1), jnp.float32, math.log(0.3), math.log(3.0)))
    col_scale = jnp.exp(jax.random.uniform(key_cols, (1, D), jnp.float32, math.log(0.3), math.log(3.0)))
    base_draw = jax.random.normal(key_main, (TOKENS, D), jnp.float32)
    return (base_draw * row_scale * col_scale).astype(jnp.bfloat16)


def draw_key_tiles(key, part):
    key_base = jax.random.fold_in(key, 21)
    scores = jax.random.randint(key_base, (WINDOWS, NB, TW), 0, 1 << 20) * TW + jnp.arange(TW, dtype=jnp.int32)
    ranked = jnp.argsort(scores, axis=-1)[:, :, :CAP].astype(jnp.int32)
    slot_ids = jnp.arange(NB, dtype=jnp.int32)
    offset = (slot_ids // 2 + 1) * (1 - 2 * (slot_ids % 2))
    source = (jnp.arange(WINDOWS, dtype=jnp.int32)[:, None] + offset[None, :] + NB * WINDOWS) % WINDOWS
    return (source[:, :, None] * TW + ranked).reshape(WINDOWS, NB * CAP).astype(jnp.int32)


def draw_key_count(key, part):
    key_base = jax.random.fold_in(key, 31)
    counts = jax.random.randint(jax.random.fold_in(key_base, 1), (WINDOWS,), 4 * CAP, NB * CAP + 1)
    full_one = jax.random.randint(jax.random.fold_in(key_base, 2), (), 0, WINDOWS)
    return jnp.where(jnp.arange(WINDOWS) == full_one, NB * CAP, counts).astype(jnp.int32)


def draw_strip_rows(key, part):
    key_base = jax.random.fold_in(key, 41)
    counts = jax.random.randint(jax.random.fold_in(key_base, 1), (WINDOWS,), OV // 4, OV + 1)
    full_one = jax.random.randint(jax.random.fold_in(key_base, 2), (), 0, WINDOWS)
    return jnp.where(jnp.arange(WINDOWS) == full_one, OV, counts).astype(jnp.int32)


def levels(stream_key, dims, pieces, smallest, largest):
    loudness = 1.0
    for dim, blocks in pieces:
        steps = jax.random.uniform(jax.random.fold_in(jax.random.fold_in(stream_key, 6), dim), (blocks,), jnp.float32, smallest / len(pieces), largest / len(pieces))
        loudness = loudness * jnp.repeat(jnp.exp(steps), dims[dim] // blocks).reshape((-1,) + (1,) * (len(dims) - 1 - dim))
    return loudness


def normal_values(own_key, dims, deviation, bound, pieces=(), kind=jnp.bfloat16):
    entries = jax.random.normal(own_key, dims, jnp.float32) * deviation
    if len(pieces) > 0:
        entries = levels(own_key, dims, pieces, -0.22, 0.18) * entries
    return jnp.clip(entries, min=-bound, max=bound).astype(kind)


def setup_inputs(seed: int = 0) -> dict:
    splits = jax.random.split(jax.random.key(seed), 11)
    return {
        "latents": draw_latents(jax.random.fold_in(splits[10], 71), 0),
        "modulation": normal_values(splits[1], (3, D), 0.5, 2.5, (), jnp.float32),
        "qkv_weight": normal_values(splits[2], (D, 3, D), D ** -0.5, 0.109375, ((2, 8),)),
        "qkv_bias": normal_values(splits[3], (3, D), 0.5, 3.0, ((1, 8),), jnp.float32),
        "norm_gain": jnp.clip(jnp.exp(jax.random.uniform(splits[4], (2, HEAD_DIM), jnp.float32, math.log(1.0), math.log(2.5))), 1.0, 2.5),
        "out_weight": normal_values(splits[5], (D, D), D ** -0.5, 0.109375, ((0, 8),)),
        "out_bias": normal_values(splits[6], (D,), 0.5, 3.0, (), jnp.float32),
        "key_tiles": draw_key_tiles(jax.random.fold_in(splits[10], 71), 0),
        "key_count": draw_key_count(jax.random.fold_in(splits[10], 71), 0),
        "strip_rows": draw_strip_rows(jax.random.fold_in(splits[10], 71), 0),
    }


def modulate(token_rows, modulation):
    rows_wide = token_rows.astype(jnp.float32)
    row_mean = lax.optimization_barrier(jnp.mean(rows_wide, axis=-1, keepdims=True))
    centred = rows_wide - row_mean
    spread = lax.optimization_barrier(jnp.mean(centred * centred, axis=-1, keepdims=True))
    normed = centred * lax.rsqrt(spread + 1e-06)
    return ((1.0 + modulation[1]) * normed + modulation[0]).astype(jnp.bfloat16)

def head_norm(raw_proj, norm_gain, head_count):
    row_total = raw_proj.shape[0]
    split_heads = raw_proj.reshape(row_total, 3, head_count, norm_gain.shape[1])
    pair_heads = split_heads[:, :2]
    mean_square = lax.optimization_barrier(jnp.mean(pair_heads * pair_heads, axis=-1, keepdims=True))
    pair_heads = pair_heads * lax.rsqrt(mean_square + 1e-06) * norm_gain[None, :, None, :]
    joined = jnp.concatenate([pair_heads, split_heads[:, 2:]], axis=1)
    return joined.reshape(row_total, 3, head_count * norm_gain.shape[1]).astype(jnp.bfloat16)

def attend(queries, key_rows, values, live_keys, head_count):
    features = queries.shape[1]
    head_dim = features // head_count
    query_heads = queries.reshape(-1, head_count, head_dim).astype(jnp.float32)
    key_heads = key_rows.reshape(-1, head_count, head_dim).astype(jnp.float32)
    value_heads = values.reshape(-1, head_count, head_dim).astype(jnp.float32)
    scores = jnp.einsum('qhd,khd->hqk', query_heads, key_heads) * head_dim ** (-0.5)
    weights = jnp.where(live_keys[None, None, :], jnp.exp(scores), jnp.float32(0.0))
    denominator = lax.optimization_barrier(jnp.sum(weights, axis=-1))
    rounded = lax.optimization_barrier(weights.astype(jnp.bfloat16))
    mixed = jnp.einsum('hqk,khd->qhd', rounded.astype(jnp.float32), value_heads)
    return (mixed / jnp.transpose(denominator)[:, :, None]).reshape(-1, features).astype(jnp.bfloat16)

def reference(latents, modulation, qkv_weight, qkv_bias, norm_gain, out_weight, out_bias, key_tiles, key_count, strip_rows):
    window_rows = TW * TILE
    flat_weight = qkv_weight.reshape(D, 3 * D)
    latent_windows = latents.reshape(WINDOWS, window_rows, D)

    def project(token_rows):
        raw_proj = jnp.dot(modulate(token_rows, modulation), flat_weight, preferred_element_type=jnp.float32)
        raw_proj = raw_proj.reshape(-1, 3, D) + qkv_bias
        return head_norm(raw_proj, norm_gain, HEADS)
    qkv_rows = lax.map(project, latent_windows)
    all_tiles = qkv_rows.reshape(WINDOWS * TW, TILE, 3, D)

    def window(window_index):
        own_tiles = window_index * TW + jnp.arange(TW, dtype=jnp.int32)
        chosen = jnp.concatenate([own_tiles, key_tiles[window_index]])
        picked = jnp.take(all_tiles, chosen, axis=0).reshape(-1, 3, D)
        live_keys = jnp.arange(picked.shape[0], dtype=jnp.int32) // TILE < TW + key_count[window_index]
        queries = qkv_rows[window_index][:, 0]
        attended = attend(queries, picked[:, 1], picked[:, 2], live_keys, HEADS)
        return jnp.dot(attended, out_weight, preferred_element_type=jnp.float32)
    projected = lax.map(window, jnp.arange(WINDOWS, dtype=jnp.int32))
    earlier = jnp.roll(projected, 1, axis=0)
    later = jnp.roll(projected, -1, axis=0)
    lead_rows = jnp.roll(strip_rows, 1)
    tail_rows = strip_rows
    row_place = jnp.arange(window_rows, dtype=jnp.int32)
    top_index = jnp.clip(window_rows - lead_rows[:, None] + row_place[None, :], 0, window_rows - 1)
    bottom_index = jnp.clip(row_place[None, :] - window_rows + tail_rows[:, None], 0, window_rows - 1)
    from_prev = jax.vmap(lambda source_rows, picks: jnp.take(source_rows, picks, axis=0))(earlier, top_index)
    from_next = jax.vmap(lambda source_rows, picks: jnp.take(source_rows, picks, axis=0))(later, bottom_index)
    in_top = (row_place[None, :] < lead_rows[:, None])[:, :, None]
    in_bottom = (row_place[None, :] >= window_rows - tail_rows[:, None])[:, :, None]
    blended_proj = jnp.where(in_top, (projected + from_prev) * 0.5, jnp.where(in_bottom, (projected + from_next) * 0.5, projected))
    result = latent_windows.astype(jnp.float32) + modulation[2] * (blended_proj + out_bias)
    return result.reshape(TOKENS, D).astype(jnp.bfloat16)
```

```python
import functools
import math

import jax
import jax.numpy as jnp
from jax import lax
from jax.experimental import pallas as pl
from jax.experimental.pallas import tpu as pltpu
from jax.sharding import PartitionSpec as P

TILE = 128
TW = 4
NB = 8
OV = 64
ROWS = 64
D = 3072
HD = 128
HEADS = 3
LW = HEADS * HD
WINDOWS = 32
GROUPS = 8
MIB = 1 << 20
SMEM = functools.partial(pl.BlockSpec, memory_space=pltpu.SMEM)
VMEM = functools.partial(pl.BlockSpec, memory_space=pltpu.VMEM)


def along_win(value, steps):
    return lax.ppermute(value, "win", [(i, (i + steps) % WINDOWS) for i in range(WINDOWS)])


def to_y(value, steps):
    return lax.ppermute(value, "head", [(h, ((h // 2 + steps) % 4) * 2 + h % 2) for h in range(GROUPS)])


def swap_core(value):
    return lax.ppermute(value, "head", [(h, h ^ 1) for h in range(GROUPS)])


def strip_pairs(bottom_core):
    pairs = []
    for w in range(WINDOWS):
        for h in range(GROUPS):
            y, c = h // 2, h % 2
            if c == bottom_core:
                pairs.append((w * GROUPS + h, (w + 1) % WINDOWS * GROUPS + 2 * y))
            else:
                pairs.append((w * GROUPS + h, (w - 1) % WINDOWS * GROUPS + 2 * y + 1))
    return pairs


def project_kernel(parts, *refs):
    lat = refs[:parts]
    modulation, weight, bias, gain, kv_ref, q_ref, mod_ref = refs[parts:]
    step = pl.program_id(0)

    @pl.when(step == 0)
    def _():
        for i in range(parts):

            def body(g, carry, i=i):
                rows = pl.ds(pl.multiple_of(g * 16, 16), 16)
                wide = lat[i][rows, :].astype(jnp.float32)
                mean = jnp.sum(wide, axis=-1, keepdims=True) * (1.0 / D)
                centred = wide - mean
                spread = jnp.sum(centred * centred, axis=-1, keepdims=True) * (1.0 / D)
                normed = centred * lax.rsqrt(spread + 1e-06)
                out = (1.0 + modulation[1:2, :]) * normed + modulation[0:1, :]
                mod_ref[pl.ds(pl.multiple_of(i * ROWS + g * 16, 16), 16), :] = out.astype(jnp.bfloat16)
                return carry

            lax.fori_loop(0, ROWS // 16, body, 0)

    raw = jnp.dot(mod_ref[...], weight[0], preferred_element_type=jnp.float32)

    def normed_heads(raw, which):
        out = []
        for h in range(HEADS):
            part = raw[:, h * HD : (h + 1) * HD]
            mean_square = jnp.sum(part * part, axis=-1, keepdims=True) * (1.0 / HD)
            out.append((part * lax.rsqrt(mean_square + 1e-06) * gain[which : which + 1, :]).astype(jnp.bfloat16))
        return out

    @pl.when(step == 0)
    def _():
        for h, part in enumerate(normed_heads(raw + bias[1:2, :], 1)):
            kv_ref[:, h * HD : (h + 1) * HD] = part

    @pl.when(step == 1)
    def _():
        kv_ref[:, LW:] = (raw + bias[2:3, :]).astype(jnp.bfloat16)

    @pl.when(step == 2)
    def _():
        for h, part in enumerate(normed_heads(raw + bias[0:1, :], 0)):
            q_ref[:, h * HD : (h + 1) * HD] = part


def project(lat, modulation, weight, bias, gain):
    parts = len(lat)
    rows = parts * ROWS
    whole = lambda shape: pl.BlockSpec(shape, lambda c: (0,) * len(shape))
    return pl.pallas_call(
        functools.partial(project_kernel, parts),
        grid=(3,),
        in_specs=[whole((ROWS, D))] * parts
        + [
            whole((3, D)),
            pl.BlockSpec((1, D, LW), lambda c: ((c + 1) % 3, 0, 0)),
            whole((3, LW)),
            whole((2, HD)),
        ],
        out_specs=[whole((rows, 2 * LW)), whole((rows, LW))],
        out_shape=[
            jax.ShapeDtypeStruct((rows, 2 * LW), jnp.bfloat16),
            jax.ShapeDtypeStruct((rows, LW), jnp.bfloat16),
        ],
        scratch_shapes=[pltpu.VMEM((rows, D), jnp.bfloat16)],
        compiler_params=pltpu.CompilerParams(vmem_limit_bytes=24 * MIB),
        cost_estimate=pl.CostEstimate(
            flops=2 * rows * D * 3 * LW, bytes_accessed=3 * D * LW * 2 + rows * D * 2, transcendentals=0
        ),
        name="project",
    )(*lat, modulation, weight, bias, gain)


def pick_tile(dst, row, chunks, place):
    a, b, c = chunks

    @pl.when(place == 0)
    def _():
        dst[row : row + TILE, :] = a[...]

    @pl.when(jnp.logical_or(place == 1, place == 2))
    def _():
        dst[row : row + TILE, :] = b[pl.ds(pl.multiple_of((place - 1) * TILE, TILE), TILE), :]

    @pl.when(place == 3)
    def _():
        dst[row : row + TILE, :] = c[...]


def select_kernel(place, a, b, c, out):
    for k in range(2):
        pick_tile(out, k * TILE, (a, b, c), place[k])


def select_tiles(place, chunks):
    return pl.pallas_call(
        select_kernel,
        in_specs=[SMEM()] + [VMEM()] * 3,
        out_specs=VMEM(),
        out_shape=jax.ShapeDtypeStruct((2 * TILE, 2 * LW), jnp.bfloat16),
        cost_estimate=pl.CostEstimate(flops=0, bytes_accessed=1 * MIB, transcendentals=0),
        name="select_tiles",
    )(place, *chunks)


def accumulate(kv, q_block, live, num, den, first):
    scale = HD**-0.5 * math.log2(math.e)
    for h in range(HEADS):
        cols = slice(h * HD, (h + 1) * HD)
        scores = lax.dot_general(
            q_block(cols), kv[:, cols], (((1,), (1,)), ((), ())), preferred_element_type=jnp.float32
        )
        weights = jnp.exp2(scores * scale)
        parts = []
        for t in range(weights.shape[1] // TILE):
            w = weights[:, t * TILE : (t + 1) * TILE]
            if live is not None:
                w = jnp.where(live(t), w, 0.0)
            parts.append(w)
        total = functools.reduce(jnp.add, parts)
        rounded = jnp.concatenate([w.astype(jnp.bfloat16) for w in parts], axis=1)
        mixed = jnp.dot(rounded, kv[:, LW + h * HD : LW + (h + 1) * HD], preferred_element_type=jnp.float32)
        if first:
            num[0][:, cols] = mixed
            den[0][:, cols] = total
        else:
            num[0][:, cols] = num[1][:, cols] + mixed
            den[0][:, cols] = den[1][:, cols] + total


QB = 256


def own_kernel(q, a, b, c, num, den, kbuf):
    @pl.when(pl.program_id(0) == 0)
    def _():
        kbuf[0:TILE, :] = a[...]
        kbuf[TILE : 3 * TILE, :] = b[...]
        kbuf[3 * TILE :, :] = c[...]

    accumulate(kbuf, lambda cols: q[:, cols], None, (num,), (den,), True)


def hop_kernel(base, place, count, q, la, lb, lc, ra, rb, rc, num_in, den_in, num, den, kbuf):
    @pl.when(pl.program_id(0) == 0)
    def _():
        for k in range(2):
            pick_tile(kbuf, k * TILE, (la, lb, lc), place[base + k])
            pick_tile(kbuf, (2 + k) * TILE, (ra, rb, rc), place[base + 2 + k])

    live = lambda t: base + t < count[0]
    accumulate(kbuf, lambda cols: q[:, cols], live, (num, num_in), (den, den_in), False)


def rows_spec(width):
    return pl.BlockSpec((QB, width), lambda i: (i, 0))


def whole_spec(shape):
    return pl.BlockSpec(shape, lambda i: (0,) * len(shape))


ATT_COST = pl.CostEstimate(flops=4 * 512 * 512 * LW, bytes_accessed=5 * MIB, transcendentals=512 * 512 * HEADS)
ACC = [jax.ShapeDtypeStruct((512, LW), jnp.float32)] * 2
KBUF = [pltpu.VMEM((4 * TILE, 2 * LW), jnp.bfloat16)]
CHUNK_SPECS = [whole_spec((n, 2 * LW)) for n in (TILE, 2 * TILE, TILE)]


def attend_own(q, chunks):
    return pl.pallas_call(
        own_kernel,
        grid=(512 // QB,),
        in_specs=[rows_spec(LW)] + CHUNK_SPECS,
        out_specs=[rows_spec(LW)] * 2,
        out_shape=ACC,
        scratch_shapes=KBUF,
        compiler_params=pltpu.CompilerParams(vmem_limit_bytes=24 * MIB),
        cost_estimate=ATT_COST,
        name="attend_own",
    )(q, *chunks)


def attend_hop(hop, place, count, q, left, right, num, den):
    return pl.pallas_call(
        functools.partial(hop_kernel, 4 * (hop - 1)),
        grid=(512 // QB,),
        in_specs=[SMEM(), SMEM(), rows_spec(LW)] + CHUNK_SPECS * 2 + [rows_spec(LW)] * 2,
        out_specs=[rows_spec(LW)] * 2,
        out_shape=ACC,
        scratch_shapes=KBUF,
        compiler_params=pltpu.CompilerParams(vmem_limit_bytes=24 * MIB),
        cost_estimate=ATT_COST,
        name="attend_hop",
    )(place, count, q, *left, *right, num, den)


def last_kernel(base, strip, count, q, left, right, num_in, den_in, own, sib, edge_a, edge_b, kbuf, num, den):
    kbuf[0 : 2 * TILE, :] = left[...]
    kbuf[2 * TILE :, :] = right[...]
    live = lambda t: base + t < count[0]
    for half in range(512 // QB):
        rows = slice(half * QB, (half + 1) * QB)
        accumulate(
            kbuf,
            lambda cols: q[rows, cols],
            live,
            (num, num_in.at[rows, :]),
            (den, den_in.at[rows, :]),
            False,
        )
        for h in range(HEADS):
            cols = slice(h * HD, (h + 1) * HD)
            total = jnp.sum(den[:, cols], axis=-1, keepdims=True)
            out = (num[:, cols] / total).astype(jnp.bfloat16)
            for t in range(QB // TILE):
                at = (half * (QB // TILE) + t) * ROWS
                own[at : at + ROWS, cols] = out[t * TILE : t * TILE + ROWS]
                sib[at : at + ROWS, cols] = out[t * TILE + ROWS : (t + 1) * TILE]
    edge_a[...] = sib[pl.ds(pl.multiple_of(strip[0] * ROWS, ROWS), ROWS), :]
    edge_b[...] = own[pl.ds(pl.multiple_of(strip[1] * ROWS, ROWS), ROWS), :]


def attend_last(strip, count, q, left, right, num, den):
    half = jax.ShapeDtypeStruct((256, LW), jnp.bfloat16)
    edge = jax.ShapeDtypeStruct((ROWS, LW), jnp.bfloat16)
    return pl.pallas_call(
        functools.partial(last_kernel, 12),
        in_specs=[SMEM()] * 2 + [VMEM()] * 5,
        out_specs=[VMEM()] * 4,
        out_shape=[half, half, edge, edge],
        scratch_shapes=KBUF + [pltpu.VMEM((QB, LW), jnp.float32)] * 2,
        compiler_params=pltpu.CompilerParams(vmem_limit_bytes=24 * MIB),
        cost_estimate=ATT_COST,
        name="attend_last",
    )(strip, count, q, left, right, num, den)


NCOL = 768


def out_kernel(strip, own, sib, edge_own, edge_sib, w_own, w_sib, o0, o1, o3, o2, a_own, a_sib, e_own, e_sib):
    place, shared, top = strip[1], strip[2], strip[3]

    @pl.when(pl.program_id(0) == 0)
    def _():
        a_own[...] = own[...]
        a_sib[...] = sib[...]
        row = lax.broadcasted_iota(jnp.int32, (ROWS, 1), 0)
        low = jnp.where(top == 1, 0, OV - shared)
        keep = jnp.where(jnp.logical_and(row >= low, row < low + shared), 0.5, 1.0)
        at = pl.ds(pl.multiple_of(place * ROWS, ROWS), ROWS)
        a_own[at, :] = (own[at, :].astype(jnp.float32) * keep).astype(jnp.bfloat16)
        a_sib[at, :] = (sib[at, :].astype(jnp.float32) * keep).astype(jnp.bfloat16)
        i = lax.broadcasted_iota(jnp.int32, (ROWS, ROWS), 0)
        j = lax.broadcasted_iota(jnp.int32, (ROWS, ROWS), 1)
        offset = jnp.where(top == 1, OV - shared, shared - OV)
        shift = jnp.where(j == i + offset, 0.5, 0.0).astype(jnp.bfloat16)
        e_own[...] = jnp.dot(shift, edge_own[...], preferred_element_type=jnp.float32).astype(jnp.bfloat16)
        e_sib[...] = jnp.dot(shift, edge_sib[...], preferred_element_type=jnp.float32).astype(jnp.bfloat16)

    dot = functools.partial(jnp.dot, preferred_element_type=jnp.float32)
    main = dot(a_own[...], w_own[...]) + dot(a_sib[...], w_sib[...])
    extra = dot(e_own[...], w_own[...]) + dot(e_sib[...], w_sib[...])
    for k, ref in enumerate((o0, o1, o3, o2)):
        block = main[k * ROWS : (k + 1) * ROWS]
        ref[...] = (block + jnp.where(place == k, extra, 0.0)).astype(ref.dtype)


def out_project(strip, own, sib, edge_own, edge_sib, w_own, w_sib):
    cols = lambda rows: pl.BlockSpec((rows, NCOL), lambda i: (0, i))
    sent = jax.ShapeDtypeStruct((ROWS, D), jnp.bfloat16)
    return pl.pallas_call(
        out_kernel,
        grid=(D // NCOL,),
        in_specs=[SMEM()]
        + [whole_spec((256, LW))] * 2
        + [whole_spec((ROWS, LW))] * 2
        + [cols(LW)] * 2,
        out_specs=[cols(ROWS)] * 4,
        out_shape=[jax.ShapeDtypeStruct((ROWS, D), jnp.float32), sent, sent, sent],
        scratch_shapes=[pltpu.VMEM((256, LW), jnp.bfloat16)] * 2 + [pltpu.VMEM((ROWS, LW), jnp.bfloat16)] * 2,
        compiler_params=pltpu.CompilerParams(vmem_limit_bytes=24 * MIB),
        cost_estimate=pl.CostEstimate(flops=2 * 320 * 2 * LW * D, bytes_accessed=7 * MIB, transcendentals=0),
        name="out_project",
    )(strip, own, sib, edge_own, edge_sib, w_own, w_sib)


def shards(
    latents,
    modulation,
    qkv_weight,
    qkv_bias,
    norm_gain,
    out_weight,
    out_bias,
    key_tiles,
    key_count,
    strip_rows,
):
    head = lax.axis_index("head")
    y, core = head // 2, head % 2
    window = lax.axis_index("win")
    weight = jnp.transpose(qkv_weight, (1, 0, 2))
    args = (modulation, weight, qkv_bias, norm_gain)
    order = jnp.array([0, 1, 3, 2], jnp.int32)

    def places(tiles):
        return order[(tiles % TW - y) % 4]

    lat1, lat3 = to_y(latents, -1), to_y(latents, 1)
    lat2 = to_y(latents, 2)
    kv_a, q_a = project([latents, swap_core(latents)], *args)
    kv_b, q_b = project([lat1, swap_core(lat1), lat3, swap_core(lat3)], *args)
    kv_c, q_c = project([lat2, swap_core(lat2)], *args)
    q = jnp.concatenate([q_a, q_b, q_c], axis=0)

    place = places(key_tiles[0])
    tiles_next, tiles_prev = along_win(key_tiles, -1), along_win(key_tiles, 1)
    w_sib = swap_core(out_weight)

    right = left = (kv_a, kv_b, kv_c)
    num, den = attend_own(q, right)
    for hop in range(1, 4):
        right = tuple(along_win(chunk, 1) for chunk in right)
        left = tuple(along_win(chunk, -1) for chunk in left)
        num, den = attend_hop(hop, place, key_count, q, left, right, num, den)
    last_left = along_win(select_tiles(places(tiles_prev[0, 12:14]), left), -1)
    last_right = along_win(select_tiles(places(tiles_next[0, 14:16]), right), 1)

    shared = jnp.where(core == 0, strip_rows[(window + WINDOWS - 1) % WINDOWS], strip_rows[window])
    strip = jnp.stack(
        [
            order[(jnp.where(core == 0, 3, 0) - y) % 4],
            order[(jnp.where(core == 1, 3, 0) - y) % 4],
            shared,
            (core == 0).astype(jnp.int32),
        ]
    )
    own, sib, edge_a, edge_b = attend_last(strip, key_count, q, last_left, last_right, num, den)
    edge_own = lax.ppermute(edge_a, ("win", "head"), strip_pairs(0))
    edge_sib = lax.ppermute(edge_b, ("win", "head"), strip_pairs(1))
    sib = swap_core(sib)
    o0, o1, o3, o2 = out_project(strip, own, sib, edge_own, edge_sib, out_weight, w_sib)
    total = o0
    for part in (to_y(o1, 1), to_y(o3, -1), to_y(o2, 2)):
        total = total + part.astype(jnp.float32)
    result = latents.astype(jnp.float32) + modulation[2] * (total + out_bias)
    return result.astype(jnp.bfloat16)


def solution(mesh):
    in_specs = (
        P(("win", "head"), None),
        P(),
        P(None, None, "head"),
        P(None, "head"),
        P(),
        P("head", None),
        P(),
        P("win", None),
        P("win"),
        P(),
    )
    out_specs = P(("win", "head"), None)
    return jax.shard_map(shards, mesh=mesh, in_specs=in_specs, out_specs=out_specs, check_vma=False)
```

```python
import functools
import math

import jax
import jax.numpy as jnp
from jax import lax
from jax.experimental import pallas as pl
from jax.experimental.pallas import tpu as pltpu
from jax.sharding import PartitionSpec as P

TILE = 128
TW = 4
NB = 8
OV = 64
ROWS = 64
D = 3072
HD = 128
HEADS = 3
LW = HEADS * HD
WINDOWS = 32
GROUPS = 8
MIB = 1 << 20
BIG = 24
COST = pl.CostEstimate(flops=1, bytes_accessed=1, transcendentals=0)
SMEM = functools.partial(pl.BlockSpec, memory_space=pltpu.SMEM)
VMEM = functools.partial(pl.BlockSpec, memory_space=pltpu.VMEM)


def along_win(value, steps):
    return lax.ppermute(value, "win", [(i, (i + steps) % WINDOWS) for i in range(WINDOWS)])


def to_y(value, steps):
    return lax.ppermute(value, "head", [(h, ((h // 2 + steps) % 4) * 2 + h % 2) for h in range(GROUPS)])


def swap_core(value):
    return lax.ppermute(value, "head", [(h, h ^ 1) for h in range(GROUPS)])


def strip_pairs(bottom_core):
    pairs = []
    for w in range(WINDOWS):
        for h in range(GROUPS):
            y, c = h // 2, h % 2
            if c == bottom_core:
                pairs.append((w * GROUPS + h, (w + 1) % WINDOWS * GROUPS + 2 * y))
            else:
                pairs.append((w * GROUPS + h, (w - 1) % WINDOWS * GROUPS + 2 * y + 1))
    return pairs


def modulate_kernel(lat, modulation, out):
    for g in range(ROWS // 16):
        rows = slice(g * 16, (g + 1) * 16)
        wide = lat[rows, :].astype(jnp.float32)
        mean = jnp.sum(wide, axis=-1, keepdims=True) * (1.0 / D)
        centred = wide - mean
        spread = jnp.sum(centred * centred, axis=-1, keepdims=True) * (1.0 / D)
        normed = centred * lax.rsqrt(spread + 1e-06)
        out[rows, :] = ((1.0 + modulation[1:2, :]) * normed + modulation[0:1, :]).astype(jnp.bfloat16)


def modulate(lat, modulation):
    return pl.pallas_call(
        modulate_kernel,
        in_specs=[VMEM()] * 2,
        out_specs=VMEM(),
        out_shape=jax.ShapeDtypeStruct((ROWS, D), jnp.bfloat16),
        compiler_params=pltpu.CompilerParams(vmem_limit_bytes=BIG * MIB),
        cost_estimate=COST,
        name="modulate",
    )(lat, modulation)


def normed_heads(raw, gain):
    out = []
    for h in range(HEADS):
        part = raw[:, h * HD : (h + 1) * HD]
        mean_square = jnp.sum(part * part, axis=-1, keepdims=True) * (1.0 / HD)
        out.append((part * lax.rsqrt(mean_square + 1e-06) * gain).astype(jnp.bfloat16))
    return out


def kv_kernel(parts, carried, *refs):
    weight, bias, gain = refs[parts : parts + 3]
    carry = refs[parts + 3 : parts + 3 + carried]
    outs, mod_ref = refs[parts + 3 + carried : -1], refs[-1]
    step = pl.program_id(0)
    split = parts * ROWS - (TILE if carried else 0)

    def store(part, cols):
        outs[0][:, cols] = part[:split]
        for out in outs[1:]:
            out[TILE:, cols] = part[split:]

    @pl.when(step == 0)
    def _():
        for i in range(parts):
            mod_ref[i * ROWS : (i + 1) * ROWS, :] = refs[i][...]
        for ref, out in zip(carry, outs[1:]):
            out[0:TILE, :] = ref[...]
        raw = jnp.dot(mod_ref[...], weight[0], preferred_element_type=jnp.float32)
        for h, part in enumerate(normed_heads(raw + bias[1:2, :], gain[1:2, :])):
            store(part, slice(h * HD, (h + 1) * HD))

    @pl.when(step == 1)
    def _():
        raw = jnp.dot(mod_ref[...], weight[0], preferred_element_type=jnp.float32)
        store((raw + bias[2:3, :]).astype(jnp.bfloat16), slice(LW, 2 * LW))


def q_kernel(parts, *refs):
    weight, bias, gain, q_ref, mod_ref = refs[parts:]
    for i in range(parts):
        mod_ref[i * ROWS : (i + 1) * ROWS, :] = refs[i][...]
    raw = jnp.dot(mod_ref[...], weight[0], preferred_element_type=jnp.float32)
    for h, part in enumerate(normed_heads(raw + bias[0:1, :], gain[0:1, :])):
        q_ref[:, h * HD : (h + 1) * HD] = part


def project(kernel, first, count, mod, weight, bias, gain, carry=()):
    parts = len(mod)
    rows = parts * ROWS
    out_rows = [rows - TILE] + [2 * TILE] * len(carry) if carry else [rows]
    whole = lambda shape: pl.BlockSpec(shape, lambda c: (0,) * len(shape))
    out = pl.pallas_call(
        kernel,
        grid=(count,),
        in_specs=[whole((ROWS, D))] * parts
        + [pl.BlockSpec((1, D, LW), lambda c: (first + c, 0, 0)), whole((3, LW)), whole((2, HD))]
        + [whole((TILE, 2 * LW))] * len(carry),
        out_specs=[whole((n, count * LW)) for n in out_rows],
        out_shape=[jax.ShapeDtypeStruct((n, count * LW), jnp.bfloat16) for n in out_rows],
        scratch_shapes=[pltpu.VMEM((rows, D), jnp.bfloat16)],
        compiler_params=pltpu.CompilerParams(vmem_limit_bytes=BIG * MIB),
        cost_estimate=COST,
        name="project",
    )(*mod, weight, bias, gain, *carry)
    return out if carry else out[0]


def project_kv(mod, *args, carry=()):
    return project(functools.partial(kv_kernel, len(mod), len(carry)), 1, 2, mod, *args, carry=carry)


def project_q(mod, *args):
    return project(functools.partial(q_kernel, len(mod)), 0, 1, mod, *args)


def pick_tile(dst, row, chunks, place):
    a, b, c = chunks

    @pl.when(place == 0)
    def _():
        dst[row : row + TILE, :] = a[...]

    @pl.when(jnp.logical_or(place == 1, place == 2))
    def _():
        dst[row : row + TILE, :] = b[pl.ds(pl.multiple_of((place - 1) * TILE, TILE), TILE), :]

    @pl.when(place == 3)
    def _():
        dst[row : row + TILE, :] = c[...]


def place_of(tile, head):
    step = ((tile & 3) - (head >> 1)) & 3
    return step ^ (step >> 1)


def select_kernel(head, want_left, want_right, la, lb, lc, ra, rb, rc, left, right):
    for k in range(2):
        pick_tile(left, k * TILE, (la, lb, lc), place_of(want_left[0, 12 + k], head[0]))
        pick_tile(right, k * TILE, (ra, rb, rc), place_of(want_right[0, 14 + k], head[0]))


def select_tiles(head, want_left, want_right, left, right):
    return pl.pallas_call(
        select_kernel,
        grid=(1,),
        in_specs=[SMEM()] * 3 + chunk_specs((0, 0)) * 2,
        out_specs=[whole_spec((2 * TILE, 2 * LW))] * 2,
        out_shape=[jax.ShapeDtypeStruct((2 * TILE, 2 * LW), jnp.bfloat16)] * 2,
        compiler_params=pltpu.CompilerParams(vmem_limit_bytes=BIG * MIB),
        cost_estimate=COST,
        name="select_tiles",
    )(head, want_left, want_right, *left, *right)


def accumulate(kv, q_block, live, num, den, first):
    scale = HD**-0.5 * math.log2(math.e)
    for h in range(HEADS):
        cols = slice(h * HD, (h + 1) * HD)
        scores = lax.dot_general(
            q_block(cols), kv[:, cols], (((1,), (1,)), ((), ())), preferred_element_type=jnp.float32
        )
        weights = jnp.exp2(scores * scale)
        parts = []
        for t in range(weights.shape[1] // TILE):
            w = weights[:, t * TILE : (t + 1) * TILE]
            if live is not None:
                w = jnp.where(live(t), w, 0.0)
            parts.append(w)
        total = functools.reduce(jnp.add, parts)
        rounded = jnp.concatenate([w.astype(jnp.bfloat16) for w in parts], axis=1)
        mixed = jnp.dot(rounded, kv[:, LW + h * HD : LW + (h + 1) * HD], preferred_element_type=jnp.float32)
        if first:
            num[0][:, cols] = mixed
            den[0][:, cols] = total
        else:
            num[0][:, cols] = num[1][:, cols] + mixed
            den[0][:, cols] = den[1][:, cols] + total


QB = 256


def own_kernel(q, a, b, c, num, den, kbuf):
    @pl.when(pl.program_id(0) == 0)
    def _():
        kbuf[0:TILE, :] = a[...]
        kbuf[TILE : 3 * TILE, :] = b[...]
        kbuf[3 * TILE :, :] = c[...]

    accumulate(kbuf, lambda cols: q[:, cols], None, (num,), (den,), True)


def hop_kernel(base, head, tiles, count, q, la, lb, lc, ra, rb, rc, num_in, den_in, num, den, kbuf):
    @pl.when(pl.program_id(0) == 0)
    def _():
        for k in range(2):
            pick_tile(kbuf, k * TILE, (la, lb, lc), place_of(tiles[0, base + k], head[0]))
            pick_tile(kbuf, (2 + k) * TILE, (ra, rb, rc), place_of(tiles[0, base + 2 + k], head[0]))

    live = lambda t: base + t < count[0]
    accumulate(kbuf, lambda cols: q[:, cols], live, (num, num_in), (den, den_in), False)


def rows_spec(width):
    return pl.BlockSpec((QB, width), lambda i: (i, 0))


def whole_spec(shape):
    return pl.BlockSpec(shape, lambda i: (0,) * len(shape))


ACC = [jax.ShapeDtypeStruct((512, LW), jnp.float32)] * 2
KBUF = [pltpu.VMEM((4 * TILE, 2 * LW), jnp.bfloat16)]


def chunk_specs(halves):
    a, c = halves
    return [
        pl.BlockSpec((TILE, 2 * LW), lambda i: (a, 0)),
        pl.BlockSpec((2 * TILE, 2 * LW), lambda i: (0, 0)),
        pl.BlockSpec((TILE, 2 * LW), lambda i: (c, 0)),
    ]


def attend_own(q, chunks):
    return pl.pallas_call(
        own_kernel,
        grid=(512 // QB,),
        in_specs=[rows_spec(LW)] + chunk_specs((0, 1)),
        out_specs=[rows_spec(LW)] * 2,
        out_shape=ACC,
        scratch_shapes=KBUF,
        compiler_params=pltpu.CompilerParams(vmem_limit_bytes=BIG * MIB),
        cost_estimate=COST,
        name="attend_own",
    )(q, *chunks)


def attend_hop(hop, halves, head, tiles, count, q, left, right, num, den):
    return pl.pallas_call(
        functools.partial(hop_kernel, 4 * (hop - 1)),
        grid=(512 // QB,),
        in_specs=[SMEM()] * 3 + [rows_spec(LW)] + chunk_specs(halves) * 2 + [rows_spec(LW)] * 2,
        out_specs=[rows_spec(LW)] * 2,
        out_shape=ACC,
        scratch_shapes=KBUF,
        compiler_params=pltpu.CompilerParams(vmem_limit_bytes=BIG * MIB),
        cost_estimate=COST,
        name="attend_hop",
    )(head, tiles, count, q, *left, *right, num, den)


def last_kernel(base, head, count, q, left, right, num_in, den_in, own, sib, edge_a, edge_b, kbuf, num, den):
    step = pl.program_id(0)

    @pl.when(step == 0)
    def _():
        kbuf[0 : 2 * TILE, :] = left[...]
        kbuf[2 * TILE :, :] = right[...]

    live = lambda t: base + t < count[0]
    accumulate(kbuf, lambda cols: q[:, cols], live, (num, num_in), (den, den_in), False)
    for h in range(HEADS):
        cols = slice(h * HD, (h + 1) * HD)
        total = jnp.sum(den[:, cols], axis=-1, keepdims=True)
        out = (num[:, cols] / total).astype(jnp.bfloat16)
        for t in range(QB // TILE):
            at = pl.ds(pl.multiple_of(step * (QB // 2) + t * ROWS, ROWS), ROWS)
            own[at, cols] = out[t * TILE : t * TILE + ROWS]
            sib[at, cols] = out[t * TILE + ROWS : (t + 1) * TILE]

    @pl.when(step == 512 // QB - 1)
    def _():
        core = head[0] & 1
        edge_a[...] = sib[pl.ds(pl.multiple_of(place_of(3 * (1 - core), head[0]) * ROWS, ROWS), ROWS), :]
        edge_b[...] = own[pl.ds(pl.multiple_of(place_of(3 * core, head[0]) * ROWS, ROWS), ROWS), :]


def attend_last(head, count, q, left, right, num, den):
    half = jax.ShapeDtypeStruct((256, LW), jnp.bfloat16)
    edge = jax.ShapeDtypeStruct((ROWS, LW), jnp.bfloat16)
    return pl.pallas_call(
        functools.partial(last_kernel, 12),
        grid=(512 // QB,),
        in_specs=[SMEM()] * 2
        + [rows_spec(LW)]
        + [whole_spec((2 * TILE, 2 * LW))] * 2
        + [rows_spec(LW)] * 2,
        out_specs=[whole_spec((256, LW))] * 2 + [whole_spec((ROWS, LW))] * 2,
        out_shape=[half, half, edge, edge],
        scratch_shapes=KBUF + [pltpu.VMEM((QB, LW), jnp.float32)] * 2,
        compiler_params=pltpu.CompilerParams(vmem_limit_bytes=BIG * MIB),
        cost_estimate=COST,
        name="attend_last",
    )(head, count, q, left, right, num, den)


NCOL = 768


def out_kernel(head, window, strips, own, sib, edge_own, edge_sib, w_own, w_sib, o0, o1, o3, o2, a_own, a_sib, e_own, e_sib):
    core = head[0] & 1
    place = place_of(3 * core, head[0])
    shared = strips[(window[0] + core + WINDOWS - 1) & (WINDOWS - 1)]
    top = 1 - core

    @pl.when(pl.program_id(0) == 0)
    def _():
        a_own[...] = own[...]
        a_sib[...] = sib[...]
        row = lax.broadcasted_iota(jnp.int32, (ROWS, 1), 0)
        low = jnp.where(top == 1, 0, OV - shared)
        keep = jnp.where(jnp.logical_and(row >= low, row < low + shared), 0.5, 1.0)
        at = pl.ds(pl.multiple_of(place * ROWS, ROWS), ROWS)
        a_own[at, :] = (own[at, :].astype(jnp.float32) * keep).astype(jnp.bfloat16)
        a_sib[at, :] = (sib[at, :].astype(jnp.float32) * keep).astype(jnp.bfloat16)
        i = lax.broadcasted_iota(jnp.int32, (ROWS, ROWS), 0)
        j = lax.broadcasted_iota(jnp.int32, (ROWS, ROWS), 1)
        offset = jnp.where(top == 1, OV - shared, shared - OV)
        shift = jnp.where(j == i + offset, 0.5, 0.0).astype(jnp.bfloat16)
        e_own[...] = jnp.dot(shift, edge_own[...], preferred_element_type=jnp.float32).astype(jnp.bfloat16)
        e_sib[...] = jnp.dot(shift, edge_sib[...], preferred_element_type=jnp.float32).astype(jnp.bfloat16)

    dot = functools.partial(jnp.dot, preferred_element_type=jnp.float32)
    main = dot(a_own[...], w_own[...]) + dot(a_sib[...], w_sib[...])
    extra = dot(e_own[...], w_own[...]) + dot(e_sib[...], w_sib[...])
    for k, ref in enumerate((o0, o1, o3, o2)):
        block = main[k * ROWS : (k + 1) * ROWS]
        ref[...] = (block + jnp.where(place == k, extra, 0.0)).astype(ref.dtype)


def out_project(head, window, strips, own, sib, edge_own, edge_sib, w_own, w_sib):
    cols = lambda rows: pl.BlockSpec((rows, NCOL), lambda i: (0, i))
    sent = jax.ShapeDtypeStruct((ROWS, D), jnp.bfloat16)
    return pl.pallas_call(
        out_kernel,
        grid=(D // NCOL,),
        in_specs=[SMEM()] * 3
        + [whole_spec((256, LW))] * 2
        + [whole_spec((ROWS, LW))] * 2
        + [cols(LW)] * 2,
        out_specs=[cols(ROWS)] * 4,
        out_shape=[jax.ShapeDtypeStruct((ROWS, D), jnp.float32), sent, sent, sent],
        scratch_shapes=[pltpu.VMEM((256, LW), jnp.bfloat16)] * 2 + [pltpu.VMEM((ROWS, LW), jnp.bfloat16)] * 2,
        compiler_params=pltpu.CompilerParams(vmem_limit_bytes=24 * MIB),
        cost_estimate=COST,
        name="out_project",
    )(head, window, strips, own, sib, edge_own, edge_sib, w_own, w_sib)


def shards(
    latents,
    modulation,
    qkv_weight,
    qkv_bias,
    norm_gain,
    out_weight,
    out_bias,
    key_tiles,
    key_count,
    strip_rows,
):
    head = lax.axis_index("head").reshape(1)
    window = lax.axis_index("win").reshape(1)
    weight = jnp.transpose(qkv_weight, (1, 0, 2))
    args = (weight, qkv_bias, norm_gain)
    barrier = lax.optimization_barrier

    mod0 = modulate(latents, modulation)
    sib0 = swap_core(mod0)
    mod1, mod3 = to_y(mod0, -1), to_y(mod0, 1)
    mod2 = to_y(mod0, 2)
    kv_a = project_kv([mod0, sib0], *args)
    ra1, la1 = along_win(kv_a, 1), along_win(kv_a, -1)
    mod1, mod3, mod2, ra1, la1, wanted = barrier((mod1, mod3, mod2, ra1, la1, key_tiles))
    sib1, sib3, sib2 = swap_core(mod1), swap_core(mod3), swap_core(mod2)
    tiles_next, tiles_prev = along_win(wanted, -1), along_win(wanted, 1)
    sib1, sib3, sib2, tiles_next, tiles_prev = barrier((sib1, sib3, sib2, tiles_next, tiles_prev))
    kv_b, right_ac, left_ac = project_kv([mod1, sib1, mod3, sib3, mod2, sib2], *args, carry=(ra1, la1))
    rb1, lb1 = along_win(kv_b, 1), along_win(kv_b, -1)
    rac2, lac2 = along_win(right_ac, 1), along_win(left_ac, -1)
    kv_b, w_sent = barrier((kv_b, out_weight))
    w_sib = swap_core(w_sent)
    q = project_q([mod0, sib0, mod1, sib1, mod3, sib3, mod2, sib2], *args)
    hop_args = (head, key_tiles, key_count, q)
    num, den = attend_own(q, (kv_a, kv_b, right_ac))
    rb1, lb1, num, den, w_sib = barrier((rb1, lb1, num, den, w_sib))
    rb2, lb2 = along_win(rb1, 1), along_win(lb1, -1)
    rac3, lac3 = along_win(rac2, 1), along_win(lac2, -1)
    num, den = attend_hop(1, (0, 1), *hop_args, (la1, lb1, lac2), (ra1, rb1, rac2), num, den)
    rb2, lb2, num, den = barrier((rb2, lb2, num, den))
    rb3, lb3 = along_win(rb2, 1), along_win(lb2, -1)
    rc3, lc3 = along_win(rac3[TILE:], 1), along_win(lac3[TILE:], -1)
    num, den = attend_hop(2, (0, 1), *hop_args, (lac2, lb2, lac3), (rac2, rb2, rac3), num, den)
    rb3, lb3, rc3, lc3, num, den = barrier((rb3, lb3, rc3, lc3, num, den))
    right, left = (rac3, rb3, rc3), (lac3, lb3, lc3)
    last_left, last_right = select_tiles(head, tiles_prev, tiles_next, left, right)
    last_left, last_right = along_win(last_left, -1), along_win(last_right, 1)
    num, den = attend_hop(3, (0, 0), *hop_args, right=right, left=left, num=num, den=den)

    own, sib, edge_a, edge_b = attend_last(head, key_count, q, last_left, last_right, num, den)
    edge_own = lax.ppermute(edge_a, ("win", "head"), strip_pairs(0))
    edge_sib = lax.ppermute(edge_b, ("win", "head"), strip_pairs(1))
    sib = swap_core(sib)
    o0, o1, o3, o2 = out_project(head, window, strip_rows, own, sib, edge_own, edge_sib, out_weight, w_sib)
    total = o0
    for part in (to_y(o1, 1), to_y(o3, -1), to_y(o2, 2)):
        total = total + part.astype(jnp.float32)
    result = latents.astype(jnp.float32) + modulation[2] * (total + out_bias)
    return result.astype(jnp.bfloat16)


def solution(mesh):
    in_specs = (
        P(("win", "head"), None),
        P(),
        P(None, None, "head"),
        P(None, "head"),
        P(),
        P("head", None),
        P(),
        P("win", None),
        P("win"),
        P(),
    )
    out_specs = P(("win", "head"), None)
    return jax.shard_map(shards, mesh=mesh, in_specs=in_specs, out_specs=out_specs, check_vma=False)
```

```python
import functools
import math

import jax
import jax.numpy as jnp
from jax import lax
from jax.experimental import pallas as pl
from jax.experimental.pallas import tpu as pltpu
from jax.sharding import PartitionSpec as P

TILE = 128
TW = 4
NB = 8
OV = 64
ROWS = 64
NOTE = 16
D = 3072
HD = 128
HEADS = 3
LW = HEADS * HD
WINDOWS = 32
GROUPS = 8
MIB = 1 << 20
BIG = 24
COST = pl.CostEstimate(flops=1, bytes_accessed=1, transcendentals=0)
SMEM = functools.partial(pl.BlockSpec, memory_space=pltpu.SMEM)
VMEM = functools.partial(pl.BlockSpec, memory_space=pltpu.VMEM)


def along_win(value, steps):
    return lax.ppermute(value, "win", [(i, (i + steps) % WINDOWS) for i in range(WINDOWS)])


def to_y(value, steps):
    return lax.ppermute(value, "head", [(h, ((h // 2 + steps) % 4) * 2 + h % 2) for h in range(GROUPS)])


def swap_core(value):
    return lax.ppermute(value, "head", [(h, h ^ 1) for h in range(GROUPS)])


def strip_pairs(bottom_core):
    pairs = []
    for w in range(WINDOWS):
        for h in range(GROUPS):
            y, c = h // 2, h % 2
            if c == bottom_core:
                pairs.append((w * GROUPS + h, (w + 1) % WINDOWS * GROUPS + 2 * y))
            else:
                pairs.append((w * GROUPS + h, (w - 1) % WINDOWS * GROUPS + 2 * y + 1))
    return pairs


def modulate_kernel(lat, modulation, out):
    for g in range(ROWS // 16):
        rows = slice(g * 16, (g + 1) * 16)
        wide = lat[rows, :].astype(jnp.float32)
        mean = jnp.sum(wide, axis=-1, keepdims=True) * (1.0 / D)
        centred = wide - mean
        spread = jnp.sum(centred * centred, axis=-1, keepdims=True) * (1.0 / D)
        normed = centred * lax.rsqrt(spread + 1e-06)
        out[rows, :] = ((1.0 + modulation[1:2, :]) * normed + modulation[0:1, :]).astype(jnp.bfloat16)


def modulate(lat, modulation):
    return pl.pallas_call(
        modulate_kernel,
        in_specs=[VMEM()] * 2,
        out_specs=VMEM(),
        out_shape=jax.ShapeDtypeStruct((ROWS, D), jnp.bfloat16),
        compiler_params=pltpu.CompilerParams(vmem_limit_bytes=BIG * MIB),
        cost_estimate=COST,
        name="modulate",
    )(lat, modulation)


def normed_heads(raw, gain):
    out = []
    for h in range(HEADS):
        part = raw[:, h * HD : (h + 1) * HD]
        mean_square = jnp.sum(part * part, axis=-1, keepdims=True) * (1.0 / HD)
        out.append((part * lax.rsqrt(mean_square + 1e-06) * gain).astype(jnp.bfloat16))
    return out


def kv_kernel(parts, carried, *refs):
    weight, bias, gain = refs[parts : parts + 3]
    extra = carried or 1
    carry = refs[parts + 3 : parts + 3 + extra]
    outs, mod_ref = refs[parts + 3 + extra : -1], refs[-1]
    step = pl.program_id(0)
    split = parts * ROWS - (TILE if carried else 0)

    def store(part, cols):
        outs[0][:split, cols] = part[:split]
        for out in outs[1:]:
            out[TILE:, cols] = part[split:]

    @pl.when(step == 0)
    def _():
        for i in range(parts):
            mod_ref[i * ROWS : (i + 1) * ROWS, :] = refs[i][...]
        for ref, out in zip(carry, outs[1:]):
            out[0:TILE, :] = ref[...]
        if not carried:
            lane = lax.broadcasted_iota(jnp.int32, (NOTE, 2 * LW), 1)
            row = jnp.zeros((NOTE, 2 * LW), jnp.int32)
            for e in range(2 * NB):
                row = jnp.where(lane == e, carry[0][0, e], row)
            outs[0][split:, :] = row.astype(jnp.float32).astype(jnp.bfloat16)
        raw = jnp.dot(mod_ref[...], weight[0], preferred_element_type=jnp.float32)
        for h, part in enumerate(normed_heads(raw + bias[1:2, :], gain[1:2, :])):
            store(part, slice(h * HD, (h + 1) * HD))

    @pl.when(step == 1)
    def _():
        raw = jnp.dot(mod_ref[...], weight[0], preferred_element_type=jnp.float32)
        store((raw + bias[2:3, :]).astype(jnp.bfloat16), slice(LW, 2 * LW))


def q_kernel(parts, *refs):
    weight, bias, gain, q_ref, mod_ref = refs[parts:]
    for i in range(parts):
        mod_ref[i * ROWS : (i + 1) * ROWS, :] = refs[i][...]
    raw = jnp.dot(mod_ref[...], weight[0], preferred_element_type=jnp.float32)
    for h, part in enumerate(normed_heads(raw + bias[0:1, :], gain[0:1, :])):
        q_ref[:, h * HD : (h + 1) * HD] = part


def project(kernel, first, count, mod, weight, bias, gain, carry=(), tiles=None):
    parts = len(mod)
    rows = parts * ROWS
    out_rows = [rows - TILE] + [2 * TILE] * len(carry) if carry else [rows + (NOTE if tiles is not None else 0)]
    noted = [tiles] if tiles is not None else []
    whole = lambda shape: pl.BlockSpec(shape, lambda c: (0,) * len(shape))
    out = pl.pallas_call(
        kernel,
        grid=(count,),
        in_specs=[whole((ROWS, D))] * parts
        + [pl.BlockSpec((1, D, LW), lambda c: (first + c, 0, 0)), whole((3, LW)), whole((2, HD))]
        + [whole((TILE, 2 * LW))] * len(carry)
        + [SMEM()] * len(noted),
        out_specs=[whole((n, count * LW)) for n in out_rows],
        out_shape=[jax.ShapeDtypeStruct((n, count * LW), jnp.bfloat16) for n in out_rows],
        scratch_shapes=[pltpu.VMEM((rows, D), jnp.bfloat16)],
        compiler_params=pltpu.CompilerParams(vmem_limit_bytes=BIG * MIB),
        cost_estimate=COST,
        name="project",
    )(*mod, weight, bias, gain, *carry, *noted)
    return out if carry else out[0]


def project_kv(mod, *args, carry=(), tiles=None):
    return project(functools.partial(kv_kernel, len(mod), len(carry)), 1, 2, mod, *args, carry=carry, tiles=tiles)


def project_q(mod, *args):
    return project(functools.partial(q_kernel, len(mod)), 0, 1, mod, *args)


def pick_tile(dst, row, chunks, place):
    a, b, c = chunks

    @pl.when(place == 0)
    def _():
        dst[row : row + TILE, :] = a[...]

    @pl.when(jnp.logical_or(place == 1, place == 2))
    def _():
        dst[row : row + TILE, :] = b[pl.ds(pl.multiple_of((place - 1) * TILE, TILE), TILE), :]

    @pl.when(place == 3)
    def _():
        dst[row : row + TILE, :] = c[...]


def place_of(tile, head):
    step = ((tile & 3) - (head >> 1)) & 3
    return step ^ (step >> 1)


def select_kernel(head, want_left, want_right, la, lb, lc, ra, rb, rc, left, right):
    for k in range(2):
        pick_tile(left, k * TILE, (la, lb, lc), place_of(want_left[0, 12 + k], head[0]))
        pick_tile(right, k * TILE, (ra, rb, rc), place_of(want_right[0, 14 + k], head[0]))


def select_tiles(head, want_left, want_right, left, right):
    return pl.pallas_call(
        select_kernel,
        grid=(1,),
        in_specs=[SMEM()] * 3 + chunk_specs((0, 0)) * 2,
        out_specs=[whole_spec((2 * TILE, 2 * LW))] * 2,
        out_shape=[jax.ShapeDtypeStruct((2 * TILE, 2 * LW), jnp.bfloat16)] * 2,
        compiler_params=pltpu.CompilerParams(vmem_limit_bytes=BIG * MIB),
        cost_estimate=COST,
        name="select_tiles",
    )(head, want_left, want_right, *left, *right)


def accumulate(kv, q_block, live, num, den, first):
    scale = HD**-0.5 * math.log2(math.e)
    for h in range(HEADS):
        cols = slice(h * HD, (h + 1) * HD)
        scores = lax.dot_general(
            q_block(cols), kv[:, cols], (((1,), (1,)), ((), ())), preferred_element_type=jnp.float32
        )
        weights = jnp.exp2(scores * scale)
        parts = []
        for t in range(weights.shape[1] // TILE):
            w = weights[:, t * TILE : (t + 1) * TILE]
            if live is not None:
                w = jnp.where(live(t), w, 0.0)
            parts.append(w)
        total = functools.reduce(jnp.add, parts)
        rounded = jnp.concatenate([w.astype(jnp.bfloat16) for w in parts], axis=1)
        mixed = jnp.dot(rounded, kv[:, LW + h * HD : LW + (h + 1) * HD], preferred_element_type=jnp.float32)
        if first:
            num[0][:, cols] = mixed
            den[0][:, cols] = total
        else:
            num[0][:, cols] = num[1][:, cols] + mixed
            den[0][:, cols] = den[1][:, cols] + total


QB = 256


def own_kernel(q, a, b, c, num, den, kbuf):
    @pl.when(pl.program_id(0) == 0)
    def _():
        kbuf[0:TILE, :] = a[...]
        kbuf[TILE : 3 * TILE, :] = b[...]
        kbuf[3 * TILE :, :] = c[...]

    accumulate(kbuf, lambda cols: q[:, cols], None, (num,), (den,), True)


def hop_kernel(base, head, tiles, count, q, la, lb, lc, ra, rb, rc, num_in, den_in, num, den, kbuf):
    @pl.when(pl.program_id(0) == 0)
    def _():
        for k in range(2):
            pick_tile(kbuf, k * TILE, (la, lb, lc), place_of(tiles[0, base + k], head[0]))
            pick_tile(kbuf, (2 + k) * TILE, (ra, rb, rc), place_of(tiles[0, base + 2 + k], head[0]))

    live = lambda t: base + t < count[0]
    accumulate(kbuf, lambda cols: q[:, cols], live, (num, num_in), (den, den_in), False)


def rows_spec(width):
    return pl.BlockSpec((QB, width), lambda i: (i, 0))


def whole_spec(shape):
    return pl.BlockSpec(shape, lambda i: (0,) * len(shape))


ACC = [jax.ShapeDtypeStruct((512, LW), jnp.float32)] * 2
KBUF = [pltpu.VMEM((4 * TILE, 2 * LW), jnp.bfloat16)]


def chunk_specs(halves):
    a, c = halves
    return [
        pl.BlockSpec((TILE, 2 * LW), lambda i: (a, 0)),
        pl.BlockSpec((2 * TILE, 2 * LW), lambda i: (0, 0)),
        pl.BlockSpec((TILE, 2 * LW), lambda i: (c, 0)),
    ]


def attend_own(q, chunks):
    return pl.pallas_call(
        own_kernel,
        grid=(512 // QB,),
        in_specs=[rows_spec(LW)] + chunk_specs((0, 1)),
        out_specs=[rows_spec(LW)] * 2,
        out_shape=ACC,
        scratch_shapes=KBUF,
        compiler_params=pltpu.CompilerParams(vmem_limit_bytes=BIG * MIB),
        cost_estimate=COST,
        name="attend_own",
    )(q, *chunks)


def attend_hop(hop, halves, head, tiles, count, q, left, right, num, den):
    return pl.pallas_call(
        functools.partial(hop_kernel, 4 * (hop - 1)),
        grid=(512 // QB,),
        in_specs=[SMEM()] * 3 + [rows_spec(LW)] + chunk_specs(halves) * 2 + [rows_spec(LW)] * 2,
        out_specs=[rows_spec(LW)] * 2,
        out_shape=ACC,
        scratch_shapes=KBUF,
        compiler_params=pltpu.CompilerParams(vmem_limit_bytes=BIG * MIB),
        cost_estimate=COST,
        name="attend_hop",
    )(head, tiles, count, q, *left, *right, num, den)


def last_kernel(base, head, count, q, left, right, num_in, den_in, own, sib, edge_a, edge_b, kbuf, num, den):
    step = pl.program_id(0)

    @pl.when(step == 0)
    def _():
        kbuf[0 : 2 * TILE, :] = left[...]
        kbuf[2 * TILE :, :] = right[...]

    live = lambda t: base + t < count[0]
    accumulate(kbuf, lambda cols: q[:, cols], live, (num, num_in), (den, den_in), False)
    for h in range(HEADS):
        cols = slice(h * HD, (h + 1) * HD)
        total = jnp.sum(den[:, cols], axis=-1, keepdims=True)
        out = (num[:, cols] / total).astype(jnp.bfloat16)
        for t in range(QB // TILE):
            at = pl.ds(pl.multiple_of(step * (QB // 2) + t * ROWS, ROWS), ROWS)
            own[at, cols] = out[t * TILE : t * TILE + ROWS]
            sib[at, cols] = out[t * TILE + ROWS : (t + 1) * TILE]

    @pl.when(step == 512 // QB - 1)
    def _():
        core = head[0] & 1
        edge_a[...] = sib[pl.ds(pl.multiple_of(place_of(3 * (1 - core), head[0]) * ROWS, ROWS), ROWS), :]
        edge_b[...] = own[pl.ds(pl.multiple_of(place_of(3 * core, head[0]) * ROWS, ROWS), ROWS), :]


def attend_last(head, count, q, left, right, num, den):
    half = jax.ShapeDtypeStruct((256, LW), jnp.bfloat16)
    edge = jax.ShapeDtypeStruct((ROWS, LW), jnp.bfloat16)
    return pl.pallas_call(
        functools.partial(last_kernel, 12),
        grid=(512 // QB,),
        in_specs=[SMEM()] * 2
        + [rows_spec(LW)]
        + [whole_spec((2 * TILE, 2 * LW))] * 2
        + [rows_spec(LW)] * 2,
        out_specs=[whole_spec((256, LW))] * 2 + [whole_spec((ROWS, LW))] * 2,
        out_shape=[half, half, edge, edge],
        scratch_shapes=KBUF + [pltpu.VMEM((QB, LW), jnp.float32)] * 2,
        compiler_params=pltpu.CompilerParams(vmem_limit_bytes=BIG * MIB),
        cost_estimate=COST,
        name="attend_last",
    )(head, count, q, left, right, num, den)


NCOL = 768


def strip_of(head, window, strips):
    core = head[0] & 1
    return place_of(3 * core, head[0]), strips[(window[0] + core + WINDOWS - 1) & (WINDOWS - 1)], 1 - core


def halve_shared(a, rows, place, shared, top):
    a[...] = rows[...]
    row = lax.broadcasted_iota(jnp.int32, (ROWS, 1), 0)
    low = jnp.where(top == 1, 0, OV - shared)
    keep = jnp.where(jnp.logical_and(row >= low, row < low + shared), 0.5, 1.0)
    at = pl.ds(pl.multiple_of(place * ROWS, ROWS), ROWS)
    a[at, :] = (rows[at, :].astype(jnp.float32) * keep).astype(jnp.bfloat16)


dot = functools.partial(jnp.dot, preferred_element_type=jnp.float32)


def out_own_kernel(head, window, strips, own, w_own, part, a_own):
    @pl.when(pl.program_id(0) == 0)
    def _():
        halve_shared(a_own, own, *strip_of(head, window, strips))

    part[...] = dot(a_own[...], w_own[...])


def out_kernel(head, window, strips, part, sib, edge_own, edge_sib, w_own, w_sib, o0, o1, o3, o2, a_sib, e_own, e_sib):
    place, shared, top = strip_of(head, window, strips)

    @pl.when(pl.program_id(0) == 0)
    def _():
        halve_shared(a_sib, sib, place, shared, top)
        i = lax.broadcasted_iota(jnp.int32, (ROWS, ROWS), 0)
        j = lax.broadcasted_iota(jnp.int32, (ROWS, ROWS), 1)
        offset = jnp.where(top == 1, OV - shared, shared - OV)
        shift = jnp.where(j == i + offset, 0.5, 0.0).astype(jnp.bfloat16)
        e_own[...] = dot(shift, edge_own[...]).astype(jnp.bfloat16)
        e_sib[...] = dot(shift, edge_sib[...]).astype(jnp.bfloat16)

    main = part[...] + dot(a_sib[...], w_sib[...])
    extra = dot(e_own[...], w_own[...]) + dot(e_sib[...], w_sib[...])
    for k, ref in enumerate((o0, o1, o3, o2)):
        block = main[k * ROWS : (k + 1) * ROWS]
        ref[...] = (block + jnp.where(place == k, extra, 0.0)).astype(ref.dtype)


def out_cols(rows):
    return pl.BlockSpec((rows, NCOL), lambda i: (0, i))


def out_own(head, window, strips, own, w_own):
    return pl.pallas_call(
        out_own_kernel,
        grid=(D // NCOL,),
        in_specs=[SMEM()] * 3 + [whole_spec((256, LW)), out_cols(LW)],
        out_specs=out_cols(256),
        out_shape=jax.ShapeDtypeStruct((256, D), jnp.float32),
        scratch_shapes=[pltpu.VMEM((256, LW), jnp.bfloat16)],
        compiler_params=pltpu.CompilerParams(vmem_limit_bytes=BIG * MIB),
        cost_estimate=COST,
        name="out_own",
    )(head, window, strips, own, w_own)


def out_project(head, window, strips, part, sib, edge_own, edge_sib, w_own, w_sib):
    sent = jax.ShapeDtypeStruct((ROWS, D), jnp.bfloat16)
    return pl.pallas_call(
        out_kernel,
        grid=(D // NCOL,),
        in_specs=[SMEM()] * 3
        + [out_cols(256), whole_spec((256, LW))]
        + [whole_spec((ROWS, LW))] * 2
        + [out_cols(LW)] * 2,
        out_specs=[out_cols(ROWS)] * 4,
        out_shape=[jax.ShapeDtypeStruct((ROWS, D), jnp.float32), sent, sent, sent],
        scratch_shapes=[pltpu.VMEM((256, LW), jnp.bfloat16)] + [pltpu.VMEM((ROWS, LW), jnp.bfloat16)] * 2,
        compiler_params=pltpu.CompilerParams(vmem_limit_bytes=BIG * MIB),
        cost_estimate=COST,
        name="out_project",
    )(head, window, strips, part, sib, edge_own, edge_sib, w_own, w_sib)


def shards(
    latents,
    modulation,
    qkv_weight,
    qkv_bias,
    norm_gain,
    out_weight,
    out_bias,
    key_tiles,
    key_count,
    strip_rows,
):
    head = lax.axis_index("head").reshape(1)
    window = lax.axis_index("win").reshape(1)
    weight = jnp.transpose(qkv_weight, (1, 0, 2))
    args = (weight, qkv_bias, norm_gain)
    barrier = lax.optimization_barrier

    mod0 = modulate(latents, modulation)
    sib0 = swap_core(mod0)
    mod1, mod3 = to_y(mod0, -1), to_y(mod0, 1)
    mod2 = to_y(mod0, 2)
    kv_a = project_kv([mod0, sib0], *args, tiles=key_tiles)
    ra1, la1 = along_win(kv_a, 1), along_win(kv_a, -1)
    mod1, mod3, mod2, ra1, la1 = barrier((mod1, mod3, mod2, ra1, la1))
    sib1, sib3, sib2 = swap_core(mod1), swap_core(mod3), swap_core(mod2)
    kv_b, right_ac, left_ac = project_kv([mod1, sib1, mod3, sib3, mod2, sib2], *args, carry=(ra1, la1))
    rb1, lb1 = along_win(kv_b, 1), along_win(kv_b, -1)
    rac2, lac2 = along_win(right_ac, 1), along_win(left_ac, -1)
    kv_b, w_sent = barrier((kv_b, out_weight))
    w_sib = swap_core(w_sent)
    q = project_q([mod0, sib0, mod1, sib1, mod3, sib3, mod2, sib2], *args)
    hop_args = (head, key_tiles, key_count, q)
    num, den = attend_own(q, (kv_a, kv_b, right_ac))
    rb1, lb1, num, den, w_sib = barrier((rb1, lb1, num, den, w_sib))
    rb2, lb2 = along_win(rb1, 1), along_win(lb1, -1)
    rac3, lac3 = along_win(rac2, 1), along_win(lac2, -1)
    num, den = attend_hop(1, (0, 1), *hop_args, (la1, lb1, lac2), (ra1, rb1, rac2), num, den)
    rb2, lb2, num, den = barrier((rb2, lb2, num, den))
    rb3, lb3 = along_win(rb2, 1), along_win(lb2, -1)
    rc3, lc3 = along_win(rac3[TILE:], 1), along_win(lac3[TILE:], -1)
    num, den = attend_hop(2, (0, 1), *hop_args, (lac2, lb2, lac3), (rac2, rb2, rac3), num, den)
    rb3, lb3, rc3, lc3, num, den = barrier((rb3, lb3, rc3, lc3, num, den))
    right, left = (rac3, rb3, rc3), (lac3, lb3, lc3)
    tiles_prev, tiles_next = (x[TILE : TILE + 1, : 2 * NB].astype(jnp.int32) for x in (ra1, la1))
    last_left, last_right = select_tiles(head, tiles_prev, tiles_next, left, right)
    last_left, last_right = along_win(last_left, -1), along_win(last_right, 1)
    num, den = attend_hop(3, (0, 0), *hop_args, right=right, left=left, num=num, den=den)

    own, sib, edge_a, edge_b = attend_last(head, key_count, q, last_left, last_right, num, den)
    edge_own = lax.ppermute(edge_a, ("win", "head"), strip_pairs(0))
    edge_sib = lax.ppermute(edge_b, ("win", "head"), strip_pairs(1))
    sib = swap_core(sib)
    part = out_own(head, window, strip_rows, own, out_weight)
    part, edge_own, edge_sib, sib = barrier((part, edge_own, edge_sib, sib))
    o0, o1, o3, o2 = out_project(head, window, strip_rows, part, sib, edge_own, edge_sib, out_weight, w_sib)
    total = o0
    for part in (to_y(o1, 1), to_y(o3, -1), to_y(o2, 2)):
        total = total + part.astype(jnp.float32)
    result = latents.astype(jnp.float32) + modulation[2] * (total + out_bias)
    return result.astype(jnp.bfloat16)


def solution(mesh):
    in_specs = (
        P(("win", "head"), None),
        P(),
        P(None, None, "head"),
        P(None, "head"),
        P(),
        P("head", None),
        P(),
        P("win", None),
        P("win"),
        P(),
    )
    out_specs = P(("win", "head"), None)
    return jax.shard_map(shards, mesh=mesh, in_specs=in_specs, out_specs=out_specs, check_vma=False)
```

```python
import functools
import math

import jax
import jax.numpy as jnp
from jax import lax
from jax.experimental import pallas as pl
from jax.experimental.pallas import tpu as pltpu
from jax.sharding import PartitionSpec as P

TILE = 128
TW = 4
NB = 8
OV = 64
ROWS = 64
NOTE = 16
D = 3072
HD = 128
HEADS = 3
LW = HEADS * HD
WINDOWS = 32
GROUPS = 8
MIB = 1 << 20
BIG = 24
COST = pl.CostEstimate(flops=1, bytes_accessed=1, transcendentals=0)
SMEM = functools.partial(pl.BlockSpec, memory_space=pltpu.SMEM)
VMEM = functools.partial(pl.BlockSpec, memory_space=pltpu.VMEM)


def along_win(value, steps):
    return lax.ppermute(value, "win", [(i, (i + steps) % WINDOWS) for i in range(WINDOWS)])


def to_y(value, steps):
    return lax.ppermute(value, "head", [(h, ((h // 2 + steps) % 4) * 2 + h % 2) for h in range(GROUPS)])


def swap_core(value):
    return lax.ppermute(value, "head", [(h, h ^ 1) for h in range(GROUPS)])


def strip_pairs(bottom_core):
    pairs = []
    for w in range(WINDOWS):
        for h in range(GROUPS):
            y, c = h // 2, h % 2
            if c == bottom_core:
                pairs.append((w * GROUPS + h, (w + 1) % WINDOWS * GROUPS + 2 * y))
            else:
                pairs.append((w * GROUPS + h, (w - 1) % WINDOWS * GROUPS + 2 * y + 1))
    return pairs


def modulate_kernel(lat, modulation, out):
    for g in range(ROWS // 16):
        rows = slice(g * 16, (g + 1) * 16)
        wide = lat[rows, :].astype(jnp.float32)
        mean = jnp.sum(wide, axis=-1, keepdims=True) * (1.0 / D)
        centred = wide - mean
        spread = jnp.sum(centred * centred, axis=-1, keepdims=True) * (1.0 / D)
        normed = centred * lax.rsqrt(spread + 1e-06)
        out[rows, :] = ((1.0 + modulation[1:2, :]) * normed + modulation[0:1, :]).astype(jnp.bfloat16)


def modulate(lat, modulation):
    return pl.pallas_call(
        modulate_kernel,
        in_specs=[VMEM()] * 2,
        out_specs=VMEM(),
        out_shape=jax.ShapeDtypeStruct((ROWS, D), jnp.bfloat16),
        compiler_params=pltpu.CompilerParams(vmem_limit_bytes=BIG * MIB),
        cost_estimate=COST,
        name="modulate",
    )(lat, modulation)


def normed_heads(raw, gain):
    out = []
    for h in range(HEADS):
        part = raw[:, h * HD : (h + 1) * HD]
        mean_square = jnp.sum(part * part, axis=-1, keepdims=True) * (1.0 / HD)
        out.append((part * lax.rsqrt(mean_square + 1e-06) * gain).astype(jnp.bfloat16))
    return out


def kv_kernel(parts, carried, *refs):
    weight, bias, gain = refs[parts : parts + 3]
    extra = carried or 1
    carry = refs[parts + 3 : parts + 3 + extra]
    outs, mod_ref = refs[parts + 3 + extra : -1], refs[-1]
    step = pl.program_id(0)
    split = parts * ROWS - (TILE if carried else 0)

    def store(part, cols):
        outs[0][:split, cols] = part[:split]
        for out in outs[1:]:
            out[TILE:, cols] = part[split:]

    @pl.when(step == 0)
    def _():
        for i in range(parts):
            mod_ref[i * ROWS : (i + 1) * ROWS, :] = refs[i][...]
        for ref, out in zip(carry, outs[1:]):
            out[0:TILE, :] = ref[...]
        if not carried:
            lane = lax.broadcasted_iota(jnp.int32, (NOTE, 2 * LW), 1)
            row = jnp.zeros((NOTE, 2 * LW), jnp.int32)
            for e in range(2 * NB):
                row = jnp.where(lane == e, carry[0][0, e], row)
            outs[0][split:, :] = row.astype(jnp.float32).astype(jnp.bfloat16)
        raw = jnp.dot(mod_ref[...], weight[0], preferred_element_type=jnp.float32)
        for h, part in enumerate(normed_heads(raw + bias[1:2, :], gain[1:2, :])):
            store(part, slice(h * HD, (h + 1) * HD))

    @pl.when(step == 1)
    def _():
        raw = jnp.dot(mod_ref[...], weight[0], preferred_element_type=jnp.float32)
        store((raw + bias[2:3, :]).astype(jnp.bfloat16), slice(LW, 2 * LW))


def q_kernel(parts, *refs):
    weight, bias, gain, q_ref, mod_ref = refs[parts:]
    for i in range(parts):
        mod_ref[i * ROWS : (i + 1) * ROWS, :] = refs[i][...]
    raw = jnp.dot(mod_ref[...], weight[0], preferred_element_type=jnp.float32)
    for h, part in enumerate(normed_heads(raw + bias[0:1, :], gain[0:1, :])):
        q_ref[:, h * HD : (h + 1) * HD] = part


def project(kernel, first, count, mod, weight, bias, gain, carry=(), tiles=None):
    parts = len(mod)
    rows = parts * ROWS
    out_rows = [rows - TILE] + [2 * TILE] * len(carry) if carry else [rows + (NOTE if tiles is not None else 0)]
    noted = [tiles] if tiles is not None else []
    whole = lambda shape: pl.BlockSpec(shape, lambda c: (0,) * len(shape))
    out = pl.pallas_call(
        kernel,
        grid=(count,),
        in_specs=[whole((ROWS, D))] * parts
        + [pl.BlockSpec((1, D, LW), lambda c: (first + c, 0, 0)), whole((3, LW)), whole((2, HD))]
        + [whole((TILE, 2 * LW))] * len(carry)
        + [SMEM()] * len(noted),
        out_specs=[whole((n, count * LW)) for n in out_rows],
        out_shape=[jax.ShapeDtypeStruct((n, count * LW), jnp.bfloat16) for n in out_rows],
        scratch_shapes=[pltpu.VMEM((rows, D), jnp.bfloat16)],
        compiler_params=pltpu.CompilerParams(vmem_limit_bytes=BIG * MIB),
        cost_estimate=COST,
        name="project",
    )(*mod, weight, bias, gain, *carry, *noted)
    return out if carry else out[0]


def project_kv(mod, *args, carry=(), tiles=None):
    return project(functools.partial(kv_kernel, len(mod), len(carry)), 1, 2, mod, *args, carry=carry, tiles=tiles)


def project_q(mod, *args):
    return project(functools.partial(q_kernel, len(mod)), 0, 1, mod, *args)


def pick_tile(dst, row, chunks, place):
    a, b, c = chunks

    @pl.when(place == 0)
    def _():
        dst[row : row + TILE, :] = a[...]

    @pl.when(jnp.logical_or(place == 1, place == 2))
    def _():
        dst[row : row + TILE, :] = b[pl.ds(pl.multiple_of((place - 1) * TILE, TILE), TILE), :]

    @pl.when(place == 3)
    def _():
        dst[row : row + TILE, :] = c[...]


def place_of(tile, head):
    step = ((tile & 3) - (head >> 1)) & 3
    return step ^ (step >> 1)


def select_kernel(head, want_left, want_right, la, lb, lc, ra, rb, rc, left, right):
    for k in range(2):
        pick_tile(left, k * TILE, (la, lb, lc), place_of(want_left[0, 12 + k], head[0]))
        pick_tile(right, k * TILE, (ra, rb, rc), place_of(want_right[0, 14 + k], head[0]))


def select_tiles(head, want_left, want_right, left, right):
    return pl.pallas_call(
        select_kernel,
        grid=(1,),
        in_specs=[SMEM()] * 3 + chunk_specs((0, 0)) * 2,
        out_specs=[whole_spec((2 * TILE, 2 * LW))] * 2,
        out_shape=[jax.ShapeDtypeStruct((2 * TILE, 2 * LW), jnp.bfloat16)] * 2,
        compiler_params=pltpu.CompilerParams(vmem_limit_bytes=BIG * MIB),
        cost_estimate=COST,
        name="select_tiles",
    )(head, want_left, want_right, *left, *right)


def accumulate(kv, q_block, live, num, den, first):
    scale = HD**-0.5 * math.log2(math.e)
    for h in range(HEADS):
        cols = slice(h * HD, (h + 1) * HD)
        scores = lax.dot_general(
            q_block(cols), kv[:, cols], (((1,), (1,)), ((), ())), preferred_element_type=jnp.float32
        )
        weights = jnp.exp2(scores * scale)
        parts = []
        for t in range(weights.shape[1] // TILE):
            w = weights[:, t * TILE : (t + 1) * TILE]
            if live is not None:
                w = jnp.where(live(t), w, 0.0)
            parts.append(w)
        total = functools.reduce(jnp.add, parts)
        rounded = jnp.concatenate([w.astype(jnp.bfloat16) for w in parts], axis=1)
        mixed = jnp.dot(rounded, kv[:, LW + h * HD : LW + (h + 1) * HD], preferred_element_type=jnp.float32)
        if first:
            num[0][:, cols] = mixed
            den[0][:, cols] = total
        else:
            num[0][:, cols] = num[1][:, cols] + mixed
            den[0][:, cols] = den[1][:, cols] + total


QB = 256


def own_kernel(q, a, b, c, num, den, kbuf):
    @pl.when(pl.program_id(0) == 0)
    def _():
        kbuf[0:TILE, :] = a[...]
        kbuf[TILE : 3 * TILE, :] = b[...]
        kbuf[3 * TILE :, :] = c[...]

    accumulate(kbuf, lambda cols: q[:, cols], None, (num,), (den,), True)


def hop_kernel(base, head, tiles, count, q, la, lb, lc, ra, rb, rc, num_in, den_in, num, den, kbuf):
    @pl.when(pl.program_id(0) == 0)
    def _():
        for k in range(2):
            pick_tile(kbuf, k * TILE, (la, lb, lc), place_of(tiles[0, base + k], head[0]))
            pick_tile(kbuf, (2 + k) * TILE, (ra, rb, rc), place_of(tiles[0, base + 2 + k], head[0]))

    live = lambda t: base + t < count[0]
    accumulate(kbuf, lambda cols: q[:, cols], live, (num, num_in), (den, den_in), False)


def rows_spec(width):
    return pl.BlockSpec((QB, width), lambda i: (i, 0))


def whole_spec(shape):
    return pl.BlockSpec(shape, lambda i: (0,) * len(shape))


ACC = [jax.ShapeDtypeStruct((512, LW), jnp.float32)] * 2
KBUF = [pltpu.VMEM((4 * TILE, 2 * LW), jnp.bfloat16)]


def chunk_specs(halves):
    a, c = halves
    return [
        pl.BlockSpec((TILE, 2 * LW), lambda i: (a, 0)),
        pl.BlockSpec((2 * TILE, 2 * LW), lambda i: (0, 0)),
        pl.BlockSpec((TILE, 2 * LW), lambda i: (c, 0)),
    ]


def attend_own(q, chunks):
    return pl.pallas_call(
        own_kernel,
        grid=(512 // QB,),
        in_specs=[rows_spec(LW)] + chunk_specs((0, 1)),
        out_specs=[rows_spec(LW)] * 2,
        out_shape=ACC,
        scratch_shapes=KBUF,
        compiler_params=pltpu.CompilerParams(vmem_limit_bytes=BIG * MIB),
        cost_estimate=COST,
        name="attend_own",
    )(q, *chunks)


def attend_hop(hop, halves, head, tiles, count, q, left, right, num, den):
    return pl.pallas_call(
        functools.partial(hop_kernel, 4 * (hop - 1)),
        grid=(512 // QB,),
        in_specs=[SMEM()] * 3 + [rows_spec(LW)] + chunk_specs(halves) * 2 + [rows_spec(LW)] * 2,
        out_specs=[rows_spec(LW)] * 2,
        out_shape=ACC,
        scratch_shapes=KBUF,
        compiler_params=pltpu.CompilerParams(vmem_limit_bytes=BIG * MIB),
        cost_estimate=COST,
        name="attend_hop",
    )(head, tiles, count, q, *left, *right, num, den)


def last_kernel(base, head, count, q, left, right, num_in, den_in, own, sib, edge_a, edge_b, kbuf, num, den):
    step = pl.program_id(0)

    @pl.when(step == 0)
    def _():
        kbuf[0 : 2 * TILE, :] = left[...]
        kbuf[2 * TILE :, :] = right[...]

    live = lambda t: base + t < count[0]
    accumulate(kbuf, lambda cols: q[:, cols], live, (num, num_in), (den, den_in), False)
    for h in range(HEADS):
        cols = slice(h * HD, (h + 1) * HD)
        total = jnp.sum(den[:, cols], axis=-1, keepdims=True)
        out = (num[:, cols] / total).astype(jnp.bfloat16)
        for t in range(QB // TILE):
            at = pl.ds(pl.multiple_of(step * (QB // 2) + t * ROWS, ROWS), ROWS)
            own[at, cols] = out[t * TILE : t * TILE + ROWS]
            sib[at, cols] = out[t * TILE + ROWS : (t + 1) * TILE]

    @pl.when(step == 512 // QB - 1)
    def _():
        core = head[0] & 1
        edge_a[...] = sib[pl.ds(pl.multiple_of(place_of(3 * (1 - core), head[0]) * ROWS, ROWS), ROWS), :]
        edge_b[...] = own[pl.ds(pl.multiple_of(place_of(3 * core, head[0]) * ROWS, ROWS), ROWS), :]


def attend_last(head, count, q, left, right, num, den):
    half = jax.ShapeDtypeStruct((256, LW), jnp.bfloat16)
    edge = jax.ShapeDtypeStruct((ROWS, LW), jnp.bfloat16)
    return pl.pallas_call(
        functools.partial(last_kernel, 12),
        grid=(512 // QB,),
        in_specs=[SMEM()] * 2
        + [rows_spec(LW)]
        + [whole_spec((2 * TILE, 2 * LW))] * 2
        + [rows_spec(LW)] * 2,
        out_specs=[whole_spec((256, LW))] * 2 + [whole_spec((ROWS, LW))] * 2,
        out_shape=[half, half, edge, edge],
        scratch_shapes=KBUF + [pltpu.VMEM((QB, LW), jnp.float32)] * 2,
        compiler_params=pltpu.CompilerParams(vmem_limit_bytes=BIG * MIB),
        cost_estimate=COST,
        name="attend_last",
    )(head, count, q, left, right, num, den)


NCOL = 768


def strip_of(head, window, strips):
    core = head[0] & 1
    return place_of(3 * core, head[0]), strips[(window[0] + core + WINDOWS - 1) & (WINDOWS - 1)], 1 - core


def halve_shared(a, rows, place, shared, top):
    a[...] = rows[...]
    row = lax.broadcasted_iota(jnp.int32, (ROWS, 1), 0)
    low = jnp.where(top == 1, 0, OV - shared)
    keep = jnp.where(jnp.logical_and(row >= low, row < low + shared), 0.5, 1.0)
    at = pl.ds(pl.multiple_of(place * ROWS, ROWS), ROWS)
    a[at, :] = (rows[at, :].astype(jnp.float32) * keep).astype(jnp.bfloat16)


dot = functools.partial(jnp.dot, preferred_element_type=jnp.float32)


def out_own_kernel(head, window, strips, own, w_own, part, a_own):
    @pl.when(pl.program_id(0) == 0)
    def _():
        halve_shared(a_own, own, *strip_of(head, window, strips))

    part[...] = dot(a_own[...], w_own[...])


def out_kernel(head, window, strips, part, sib, edge_own, edge_sib, w_own, w_sib, o0, o1, o3, o2, a_sib, e_own, e_sib):
    place, shared, top = strip_of(head, window, strips)

    @pl.when(pl.program_id(0) == 0)
    def _():
        halve_shared(a_sib, sib, place, shared, top)
        i = lax.broadcasted_iota(jnp.int32, (ROWS, ROWS), 0)
        j = lax.broadcasted_iota(jnp.int32, (ROWS, ROWS), 1)
        offset = jnp.where(top == 1, OV - shared, shared - OV)
        shift = jnp.where(j == i + offset, 0.5, 0.0).astype(jnp.bfloat16)
        e_own[...] = dot(shift, edge_own[...]).astype(jnp.bfloat16)
        e_sib[...] = dot(shift, edge_sib[...]).astype(jnp.bfloat16)

    main = part[...] + dot(a_sib[...], w_sib[...])
    extra = dot(e_own[...], w_own[...]) + dot(e_sib[...], w_sib[...])
    for k, ref in enumerate((o0, o1, o3, o2)):
        block = main[k * ROWS : (k + 1) * ROWS]
        ref[...] = (block + jnp.where(place == k, extra, 0.0)).astype(ref.dtype)


def out_cols(rows):
    return pl.BlockSpec((rows, NCOL), lambda i: (0, i))


def out_own(head, window, strips, own, w_own):
    return pl.pallas_call(
        out_own_kernel,
        grid=(D // NCOL,),
        in_specs=[SMEM()] * 3 + [whole_spec((256, LW)), out_cols(LW)],
        out_specs=out_cols(256),
        out_shape=jax.ShapeDtypeStruct((256, D), jnp.float32),
        scratch_shapes=[pltpu.VMEM((256, LW), jnp.bfloat16)],
        compiler_params=pltpu.CompilerParams(vmem_limit_bytes=BIG * MIB),
        cost_estimate=COST,
        name="out_own",
    )(head, window, strips, own, w_own)


def out_project(head, window, strips, part, sib, edge_own, edge_sib, w_own, w_sib):
    sent = jax.ShapeDtypeStruct((ROWS, D), jnp.bfloat16)
    return pl.pallas_call(
        out_kernel,
        grid=(D // NCOL,),
        in_specs=[SMEM()] * 3
        + [out_cols(256), whole_spec((256, LW))]
        + [whole_spec((ROWS, LW))] * 2
        + [out_cols(LW)] * 2,
        out_specs=[out_cols(ROWS)] * 4,
        out_shape=[jax.ShapeDtypeStruct((ROWS, D), jnp.float32), sent, sent, sent],
        scratch_shapes=[pltpu.VMEM((256, LW), jnp.bfloat16)] + [pltpu.VMEM((ROWS, LW), jnp.bfloat16)] * 2,
        compiler_params=pltpu.CompilerParams(vmem_limit_bytes=BIG * MIB),
        cost_estimate=COST,
        name="out_project",
    )(head, window, strips, part, sib, edge_own, edge_sib, w_own, w_sib)


def shards(
    latents,
    modulation,
    qkv_weight,
    qkv_bias,
    norm_gain,
    out_weight,
    out_bias,
    key_tiles,
    key_count,
    strip_rows,
):
    head = lax.axis_index("head").reshape(1)
    window = lax.axis_index("win").reshape(1)
    weight = jnp.transpose(qkv_weight, (1, 0, 2))
    args = (weight, qkv_bias, norm_gain)
    barrier = lax.optimization_barrier

    mod0 = modulate(latents, modulation)
    sib0 = swap_core(mod0)
    mod1, mod3 = to_y(mod0, -1), to_y(mod0, 1)
    mod2 = to_y(mod0, 2)
    kv_a = project_kv([mod0, sib0], *args, tiles=key_tiles)
    ra1, la1 = along_win(kv_a, 1), along_win(kv_a, -1)
    mod1, mod3, mod2, ra1, la1 = barrier((mod1, mod3, mod2, ra1, la1))
    sib1, sib3, sib2 = swap_core(mod1), swap_core(mod3), swap_core(mod2)
    kv_b, right_ac, left_ac = project_kv([mod1, sib1, mod3, sib3, mod2, sib2], *args, carry=(ra1, la1))
    rb1, lb1 = along_win(kv_b, 1), along_win(kv_b, -1)
    rac2, lac2 = along_win(right_ac, 1), along_win(left_ac, -1)
    kv_b, w_sent = barrier((kv_b, out_weight))
    w_sib = swap_core(w_sent)
    q = project_q([mod0, sib0, mod1, sib1, mod3, sib3, mod2, sib2], *args)
    hop_args = (head, key_tiles, key_count, q)
    num, den = attend_own(q, (kv_a, kv_b, right_ac))
    rb1, lb1, num, den = barrier((rb1, lb1, num, den))
    rb2, lb2 = along_win(rb1, 1), along_win(lb1, -1)
    rac3, lac3 = along_win(rac2, 1), along_win(lac2, -1)
    num, den, w_sib = barrier((num, den, w_sib))
    num, den = attend_hop(1, (0, 1), *hop_args, (la1, lb1, lac2), (ra1, rb1, rac2), num, den)
    rb2, lb2, num, den = barrier((rb2, lb2, num, den))
    rb3, lb3 = along_win(rb2, 1), along_win(lb2, -1)
    rc3, lc3 = along_win(rac3[TILE:], 1), along_win(lac3[TILE:], -1)
    num, den = attend_hop(2, (0, 1), *hop_args, (lac2, lb2, lac3), (rac2, rb2, rac3), num, den)
    rb3, lb3, rc3, lc3, num, den = barrier((rb3, lb3, rc3, lc3, num, den))
    right, left = (rac3, rb3, rc3), (lac3, lb3, lc3)
    tiles_prev, tiles_next = (x[TILE : TILE + 1, : 2 * NB].astype(jnp.int32) for x in (ra1, la1))
    last_left, last_right = select_tiles(head, tiles_prev, tiles_next, left, right)
    last_left, last_right = along_win(last_left, -1), along_win(last_right, 1)
    num, den = attend_hop(3, (0, 0), *hop_args, right=right, left=left, num=num, den=den)

    own, sib, edge_a, edge_b = attend_last(head, key_count, q, last_left, last_right, num, den)
    edge_own = lax.ppermute(edge_a, ("win", "head"), strip_pairs(0))
    edge_sib = lax.ppermute(edge_b, ("win", "head"), strip_pairs(1))
    sib = swap_core(sib)
    part = out_own(head, window, strip_rows, own, out_weight)
    part, edge_own, edge_sib, sib = barrier((part, edge_own, edge_sib, sib))
    o0, o1, o3, o2 = out_project(head, window, strip_rows, part, sib, edge_own, edge_sib, out_weight, w_sib)
    total = o0
    for part in (to_y(o1, 1), to_y(o3, -1), to_y(o2, 2)):
        total = total + part.astype(jnp.float32)
    result = latents.astype(jnp.float32) + modulation[2] * (total + out_bias)
    return result.astype(jnp.bfloat16)


def solution(mesh):
    in_specs = (
        P(("win", "head"), None),
        P(),
        P(None, None, "head"),
        P(None, "head"),
        P(),
        P("head", None),
        P(),
        P("win", None),
        P("win"),
        P(),
    )
    out_specs = P(("win", "head"), None)
    return jax.shard_map(shards, mesh=mesh, in_specs=in_specs, out_specs=out_specs, check_vma=False)
```

```python
import functools
import math

import jax
import jax.numpy as jnp
from jax import lax
from jax.experimental import pallas as pl
from jax.experimental.pallas import tpu as pltpu
from jax.sharding import PartitionSpec as P

TILE = 128
TW = 4
NB = 8
OV = 64
ROWS = 64
NOTE = 16
D = 3072
HD = 128
HEADS = 3
LW = HEADS * HD
WINDOWS = 32
GROUPS = 8
MIB = 1 << 20
BIG = 24
COST = pl.CostEstimate(flops=1, bytes_accessed=1, transcendentals=0)
SMEM = functools.partial(pl.BlockSpec, memory_space=pltpu.SMEM)
VMEM = functools.partial(pl.BlockSpec, memory_space=pltpu.VMEM)


def along_win(value, steps):
    return lax.ppermute(value, "win", [(i, (i + steps) % WINDOWS) for i in range(WINDOWS)])


def to_y(value, steps):
    return lax.ppermute(value, "head", [(h, ((h // 2 + steps) % 4) * 2 + h % 2) for h in range(GROUPS)])


def swap_core(value):
    return lax.ppermute(value, "head", [(h, h ^ 1) for h in range(GROUPS)])


def strip_pairs(bottom_core):
    pairs = []
    for w in range(WINDOWS):
        for h in range(GROUPS):
            y, c = h // 2, h % 2
            if c == bottom_core:
                pairs.append((w * GROUPS + h, (w + 1) % WINDOWS * GROUPS + 2 * y))
            else:
                pairs.append((w * GROUPS + h, (w - 1) % WINDOWS * GROUPS + 2 * y + 1))
    return pairs


def modulate_kernel(lat, modulation, out):
    for g in range(ROWS // 16):
        rows = slice(g * 16, (g + 1) * 16)
        wide = lat[rows, :].astype(jnp.float32)
        mean = jnp.sum(wide, axis=-1, keepdims=True) * (1.0 / D)
        centred = wide - mean
        spread = jnp.sum(centred * centred, axis=-1, keepdims=True) * (1.0 / D)
        normed = centred * lax.rsqrt(spread + 1e-06)
        out[rows, :] = ((1.0 + modulation[1:2, :]) * normed + modulation[0:1, :]).astype(jnp.bfloat16)


def modulate(lat, modulation):
    return pl.pallas_call(
        modulate_kernel,
        in_specs=[VMEM()] * 2,
        out_specs=VMEM(),
        out_shape=jax.ShapeDtypeStruct((ROWS, D), jnp.bfloat16),
        compiler_params=pltpu.CompilerParams(vmem_limit_bytes=BIG * MIB),
        cost_estimate=COST,
        name="modulate",
    )(lat, modulation)


def normed_heads(raw, gain):
    out = []
    for h in range(HEADS):
        part = raw[:, h * HD : (h + 1) * HD]
        mean_square = jnp.sum(part * part, axis=-1, keepdims=True) * (1.0 / HD)
        out.append((part * lax.rsqrt(mean_square + 1e-06) * gain).astype(jnp.bfloat16))
    return out


def kv_kernel(parts, carried, *refs):
    weight, bias, gain = refs[parts : parts + 3]
    extra = carried or 1
    carry = refs[parts + 3 : parts + 3 + extra]
    outs, mod_ref = refs[parts + 3 + extra : -1], refs[-1]
    step = pl.program_id(0)
    split = parts * ROWS - (TILE if carried else 0)

    def store(part, cols):
        outs[0][:split, cols] = part[:split]
        for out in outs[1:]:
            out[TILE:, cols] = part[split:]

    @pl.when(step == 0)
    def _():
        for i in range(parts):
            mod_ref[i * ROWS : (i + 1) * ROWS, :] = refs[i][...]
        for ref, out in zip(carry, outs[1:]):
            out[0:TILE, :] = ref[...]
        if not carried:
            lane = lax.broadcasted_iota(jnp.int32, (NOTE, 2 * LW), 1)
            row = jnp.zeros((NOTE, 2 * LW), jnp.int32)
            for e in range(2 * NB):
                row = jnp.where(lane == e, carry[0][0, e], row)
            outs[0][split:, :] = row.astype(jnp.float32).astype(jnp.bfloat16)
        raw = jnp.dot(mod_ref[...], weight[0], preferred_element_type=jnp.float32)
        for h, part in enumerate(normed_heads(raw + bias[1:2, :], gain[1:2, :])):
            store(part, slice(h * HD, (h + 1) * HD))

    @pl.when(step == 1)
    def _():
        raw = jnp.dot(mod_ref[...], weight[0], preferred_element_type=jnp.float32)
        store((raw + bias[2:3, :]).astype(jnp.bfloat16), slice(LW, 2 * LW))


def kv_both(step, rows, weight, bias, gain, store):
    @pl.when(step == 0)
    def _():
        raw = jnp.dot(rows[...], weight[0], preferred_element_type=jnp.float32)
        for h, part in enumerate(normed_heads(raw + bias[1:2, :], gain[1:2, :])):
            store(part, slice(h * HD, (h + 1) * HD))

    @pl.when(step == 1)
    def _():
        raw = jnp.dot(rows[...], weight[0], preferred_element_type=jnp.float32)
        store((raw + bias[2:3, :]).astype(jnp.bfloat16), slice(LW, 2 * LW))


def join_rows(dst, parts):
    for i, part in enumerate(parts):
        dst[i * ROWS : (i + 1) * ROWS, :] = part[...]


def kv_half_kernel(m1, m3, m2, weight, bias, gain, out, rows):
    step = pl.program_id(0)

    @pl.when(step == 0)
    def _():
        join_rows(rows, (m1, m3, m2))

    def store(part, cols):
        out[:, cols] = part

    kv_both(step, rows, weight, bias, gain, store)


def kv_rest_kernel(m1, m3, m2, weight, bias, gain, half, ra, la, kv_b, right, left, rows):
    step = pl.program_id(0)

    def place(values, at, cols):
        kv_b[at : at + ROWS, cols] = values[0:ROWS]
        kv_b[TILE + at : TILE + at + ROWS, cols] = values[ROWS : 2 * ROWS]
        for out in (right, left):
            out[TILE + at : TILE + at + ROWS, cols] = values[2 * ROWS :]

    @pl.when(step == 0)
    def _():
        join_rows(rows, (m1, m3, m2))
        right[0:TILE, :] = ra[...]
        left[0:TILE, :] = la[...]
        place(half[...], 0, slice(0, 2 * LW))

    kv_both(step, rows, weight, bias, gain, lambda part, cols: place(part, ROWS, cols))


def project_others(kernel, mod, weight, bias, gain, more, out_rows):
    whole = lambda shape: pl.BlockSpec(shape, lambda c: (0,) * len(shape))
    return pl.pallas_call(
        kernel,
        grid=(2,),
        in_specs=[whole((ROWS, D))] * 3
        + [pl.BlockSpec((1, D, LW), lambda c: (1 + c, 0, 0)), whole((3, LW)), whole((2, HD))]
        + [whole((n, 2 * LW)) for n, _ in more],
        out_specs=[whole((n, 2 * LW)) for n in out_rows],
        out_shape=[jax.ShapeDtypeStruct((n, 2 * LW), jnp.bfloat16) for n in out_rows],
        scratch_shapes=[pltpu.VMEM((3 * ROWS, D), jnp.bfloat16)],
        compiler_params=pltpu.CompilerParams(vmem_limit_bytes=BIG * MIB),
        cost_estimate=COST,
        name="project_others",
    )(*mod, weight, bias, gain, *(array for _, array in more))


def q_kernel(parts, *refs):
    weight, bias, gain, q_ref, mod_ref = refs[parts:]
    for i in range(parts):
        mod_ref[i * ROWS : (i + 1) * ROWS, :] = refs[i][...]
    raw = jnp.dot(mod_ref[...], weight[0], preferred_element_type=jnp.float32)
    for h, part in enumerate(normed_heads(raw + bias[0:1, :], gain[0:1, :])):
        q_ref[:, h * HD : (h + 1) * HD] = part


def project(kernel, first, count, mod, weight, bias, gain, carry=(), tiles=None):
    parts = len(mod)
    rows = parts * ROWS
    out_rows = [rows - TILE] + [2 * TILE] * len(carry) if carry else [rows + (NOTE if tiles is not None else 0)]
    noted = [tiles] if tiles is not None else []
    whole = lambda shape: pl.BlockSpec(shape, lambda c: (0,) * len(shape))
    out = pl.pallas_call(
        kernel,
        grid=(count,),
        in_specs=[whole((ROWS, D))] * parts
        + [pl.BlockSpec((1, D, LW), lambda c: (first + c, 0, 0)), whole((3, LW)), whole((2, HD))]
        + [whole((TILE, 2 * LW))] * len(carry)
        + [SMEM()] * len(noted),
        out_specs=[whole((n, count * LW)) for n in out_rows],
        out_shape=[jax.ShapeDtypeStruct((n, count * LW), jnp.bfloat16) for n in out_rows],
        scratch_shapes=[pltpu.VMEM((rows, D), jnp.bfloat16)],
        compiler_params=pltpu.CompilerParams(vmem_limit_bytes=BIG * MIB),
        cost_estimate=COST,
        name="project",
    )(*mod, weight, bias, gain, *carry, *noted)
    return out if carry else out[0]


def project_kv(mod, *args, carry=(), tiles=None):
    return project(functools.partial(kv_kernel, len(mod), len(carry)), 1, 2, mod, *args, carry=carry, tiles=tiles)


def project_q(mod, *args):
    return project(functools.partial(q_kernel, len(mod)), 0, 1, mod, *args)


def pick_tile(dst, row, chunks, place):
    a, b, c = chunks

    @pl.when(place == 0)
    def _():
        dst[row : row + TILE, :] = a[...]

    @pl.when(jnp.logical_or(place == 1, place == 2))
    def _():
        dst[row : row + TILE, :] = b[pl.ds(pl.multiple_of((place - 1) * TILE, TILE), TILE), :]

    @pl.when(place == 3)
    def _():
        dst[row : row + TILE, :] = c[...]


def place_of(tile, head):
    step = ((tile & 3) - (head >> 1)) & 3
    return step ^ (step >> 1)


def select_kernel(head, want_left, want_right, la, lb, lc, ra, rb, rc, left, right):
    for k in range(2):
        pick_tile(left, k * TILE, (la, lb, lc), place_of(want_left[0, 12 + k], head[0]))
        pick_tile(right, k * TILE, (ra, rb, rc), place_of(want_right[0, 14 + k], head[0]))


def select_tiles(head, want_left, want_right, left, right):
    return pl.pallas_call(
        select_kernel,
        grid=(1,),
        in_specs=[SMEM()] * 3 + chunk_specs((0, 0)) * 2,
        out_specs=[whole_spec((2 * TILE, 2 * LW))] * 2,
        out_shape=[jax.ShapeDtypeStruct((2 * TILE, 2 * LW), jnp.bfloat16)] * 2,
        compiler_params=pltpu.CompilerParams(vmem_limit_bytes=BIG * MIB),
        cost_estimate=COST,
        name="select_tiles",
    )(head, want_left, want_right, *left, *right)


def accumulate(kv, q_block, live, num, den, first):
    scale = HD**-0.5 * math.log2(math.e)
    for h in range(HEADS):
        cols = slice(h * HD, (h + 1) * HD)
        scores = lax.dot_general(
            q_block(cols), kv[:, cols], (((1,), (1,)), ((), ())), preferred_element_type=jnp.float32
        )
        weights = jnp.exp2(scores * scale)
        parts = []
        for t in range(weights.shape[1] // TILE):
            w = weights[:, t * TILE : (t + 1) * TILE]
            if live is not None:
                w = jnp.where(live(t), w, 0.0)
            parts.append(w)
        total = functools.reduce(jnp.add, parts)
        rounded = jnp.concatenate([w.astype(jnp.bfloat16) for w in parts], axis=1)
        mixed = jnp.dot(rounded, kv[:, LW + h * HD : LW + (h + 1) * HD], preferred_element_type=jnp.float32)
        if first:
            num[0][:, cols] = mixed
            den[0][:, cols] = total
        else:
            num[0][:, cols] = num[1][:, cols] + mixed
            den[0][:, cols] = den[1][:, cols] + total


QB = 256


def own_kernel(q, a, b, c, num, den, kbuf):
    @pl.when(pl.program_id(0) == 0)
    def _():
        kbuf[0:TILE, :] = a[...]
        kbuf[TILE : 3 * TILE, :] = b[...]
        kbuf[3 * TILE :, :] = c[...]

    accumulate(kbuf, lambda cols: q[:, cols], None, (num,), (den,), True)


def hop_kernel(base, head, tiles, count, q, la, lb, lc, ra, rb, rc, num_in, den_in, num, den, kbuf):
    @pl.when(pl.program_id(0) == 0)
    def _():
        for k in range(2):
            pick_tile(kbuf, k * TILE, (la, lb, lc), place_of(tiles[0, base + k], head[0]))
            pick_tile(kbuf, (2 + k) * TILE, (ra, rb, rc), place_of(tiles[0, base + 2 + k], head[0]))

    live = lambda t: base + t < count[0]
    accumulate(kbuf, lambda cols: q[:, cols], live, (num, num_in), (den, den_in), False)


def rows_spec(width):
    return pl.BlockSpec((QB, width), lambda i: (i, 0))


def whole_spec(shape):
    return pl.BlockSpec(shape, lambda i: (0,) * len(shape))


ACC = [jax.ShapeDtypeStruct((512, LW), jnp.float32)] * 2
KBUF = [pltpu.VMEM((4 * TILE, 2 * LW), jnp.bfloat16)]


def chunk_specs(halves):
    a, c = halves
    return [
        pl.BlockSpec((TILE, 2 * LW), lambda i: (a, 0)),
        pl.BlockSpec((2 * TILE, 2 * LW), lambda i: (0, 0)),
        pl.BlockSpec((TILE, 2 * LW), lambda i: (c, 0)),
    ]


def attend_own(q, chunks):
    return pl.pallas_call(
        own_kernel,
        grid=(512 // QB,),
        in_specs=[rows_spec(LW)] + chunk_specs((0, 1)),
        out_specs=[rows_spec(LW)] * 2,
        out_shape=ACC,
        scratch_shapes=KBUF,
        compiler_params=pltpu.CompilerParams(vmem_limit_bytes=BIG * MIB),
        cost_estimate=COST,
        name="attend_own",
    )(q, *chunks)


def attend_hop(hop, halves, head, tiles, count, q, left, right, num, den):
    return pl.pallas_call(
        functools.partial(hop_kernel, 4 * (hop - 1)),
        grid=(512 // QB,),
        in_specs=[SMEM()] * 3 + [rows_spec(LW)] + chunk_specs(halves) * 2 + [rows_spec(LW)] * 2,
        out_specs=[rows_spec(LW)] * 2,
        out_shape=ACC,
        scratch_shapes=KBUF,
        compiler_params=pltpu.CompilerParams(vmem_limit_bytes=BIG * MIB),
        cost_estimate=COST,
        name="attend_hop",
    )(head, tiles, count, q, *left, *right, num, den)


def last_kernel(base, head, count, q, left, right, num_in, den_in, own, sib, edge_a, edge_b, kbuf, num, den):
    step = pl.program_id(0)

    @pl.when(step == 0)
    def _():
        kbuf[0 : 2 * TILE, :] = left[...]
        kbuf[2 * TILE :, :] = right[...]

    live = lambda t: base + t < count[0]
    accumulate(kbuf, lambda cols: q[:, cols], live, (num, num_in), (den, den_in), False)
    for h in range(HEADS):
        cols = slice(h * HD, (h + 1) * HD)
        total = jnp.sum(den[:, cols], axis=-1, keepdims=True)
        out = (num[:, cols] / total).astype(jnp.bfloat16)
        for t in range(QB // TILE):
            at = pl.ds(pl.multiple_of(step * (QB // 2) + t * ROWS, ROWS), ROWS)
            own[at, cols] = out[t * TILE : t * TILE + ROWS]
            sib[at, cols] = out[t * TILE + ROWS : (t + 1) * TILE]

    @pl.when(step == 512 // QB - 1)
    def _():
        core = head[0] & 1
        edge_a[...] = sib[pl.ds(pl.multiple_of(place_of(3 * (1 - core), head[0]) * ROWS, ROWS), ROWS), :]
        edge_b[...] = own[pl.ds(pl.multiple_of(place_of(3 * core, head[0]) * ROWS, ROWS), ROWS), :]


def attend_last(head, count, q, left, right, num, den):
    half = jax.ShapeDtypeStruct((256, LW), jnp.bfloat16)
    edge = jax.ShapeDtypeStruct((ROWS, LW), jnp.bfloat16)
    return pl.pallas_call(
        functools.partial(last_kernel, 12),
        grid=(512 // QB,),
        in_specs=[SMEM()] * 2
        + [rows_spec(LW)]
        + [whole_spec((2 * TILE, 2 * LW))] * 2
        + [rows_spec(LW)] * 2,
        out_specs=[whole_spec((256, LW))] * 2 + [whole_spec((ROWS, LW))] * 2,
        out_shape=[half, half, edge, edge],
        scratch_shapes=KBUF + [pltpu.VMEM((QB, LW), jnp.float32)] * 2,
        compiler_params=pltpu.CompilerParams(vmem_limit_bytes=BIG * MIB),
        cost_estimate=COST,
        name="attend_last",
    )(head, count, q, left, right, num, den)


NCOL = 768


def strip_of(head, window, strips):
    core = head[0] & 1
    return place_of(3 * core, head[0]), strips[(window[0] + core + WINDOWS - 1) & (WINDOWS - 1)], 1 - core


def halve_shared(a, rows, place, shared, top):
    a[...] = rows[...]
    row = lax.broadcasted_iota(jnp.int32, (ROWS, 1), 0)
    low = jnp.where(top == 1, 0, OV - shared)
    keep = jnp.where(jnp.logical_and(row >= low, row < low + shared), 0.5, 1.0)
    at = pl.ds(pl.multiple_of(place * ROWS, ROWS), ROWS)
    a[at, :] = (rows[at, :].astype(jnp.float32) * keep).astype(jnp.bfloat16)


dot = functools.partial(jnp.dot, preferred_element_type=jnp.float32)


def out_own_kernel(head, window, strips, own, w_own, part, a_own):
    @pl.when(pl.program_id(0) == 0)
    def _():
        halve_shared(a_own, own, *strip_of(head, window, strips))

    part[...] = dot(a_own[...], w_own[...])


def out_kernel(head, window, strips, part, sib, edge_own, edge_sib, w_own, w_sib, o0, o1, o3, o2, a_sib, e_own, e_sib):
    place, shared, top = strip_of(head, window, strips)

    @pl.when(pl.program_id(0) == 0)
    def _():
        halve_shared(a_sib, sib, place, shared, top)
        i = lax.broadcasted_iota(jnp.int32, (ROWS, ROWS), 0)
        j = lax.broadcasted_iota(jnp.int32, (ROWS, ROWS), 1)
        offset = jnp.where(top == 1, OV - shared, shared - OV)
        shift = jnp.where(j == i + offset, 0.5, 0.0).astype(jnp.bfloat16)
        e_own[...] = dot(shift, edge_own[...]).astype(jnp.bfloat16)
        e_sib[...] = dot(shift, edge_sib[...]).astype(jnp.bfloat16)

    main = part[...] + dot(a_sib[...], w_sib[...])
    extra = dot(e_own[...], w_own[...]) + dot(e_sib[...], w_sib[...])
    for k, ref in enumerate((o0, o1, o3, o2)):
        block = main[k * ROWS : (k + 1) * ROWS]
        ref[...] = (block + jnp.where(place == k, extra, 0.0)).astype(ref.dtype)


def out_cols(rows):
    return pl.BlockSpec((rows, NCOL), lambda i: (0, i))


def out_own(head, window, strips, own, w_own):
    return pl.pallas_call(
        out_own_kernel,
        grid=(D // NCOL,),
        in_specs=[SMEM()] * 3 + [whole_spec((256, LW)), out_cols(LW)],
        out_specs=out_cols(256),
        out_shape=jax.ShapeDtypeStruct((256, D), jnp.float32),
        scratch_shapes=[pltpu.VMEM((256, LW), jnp.bfloat16)],
        compiler_params=pltpu.CompilerParams(vmem_limit_bytes=BIG * MIB),
        cost_estimate=COST,
        name="out_own",
    )(head, window, strips, own, w_own)


def out_project(head, window, strips, part, sib, edge_own, edge_sib, w_own, w_sib):
    sent = jax.ShapeDtypeStruct((ROWS, D), jnp.bfloat16)
    return pl.pallas_call(
        out_kernel,
        grid=(D // NCOL,),
        in_specs=[SMEM()] * 3
        + [out_cols(256), whole_spec((256, LW))]
        + [whole_spec((ROWS, LW))] * 2
        + [out_cols(LW)] * 2,
        out_specs=[out_cols(ROWS)] * 4,
        out_shape=[jax.ShapeDtypeStruct((ROWS, D), jnp.float32), sent, sent, sent],
        scratch_shapes=[pltpu.VMEM((256, LW), jnp.bfloat16)] + [pltpu.VMEM((ROWS, LW), jnp.bfloat16)] * 2,
        compiler_params=pltpu.CompilerParams(vmem_limit_bytes=BIG * MIB),
        cost_estimate=COST,
        name="out_project",
    )(head, window, strips, part, sib, edge_own, edge_sib, w_own, w_sib)


def shards(
    latents,
    modulation,
    qkv_weight,
    qkv_bias,
    norm_gain,
    out_weight,
    out_bias,
    key_tiles,
    key_count,
    strip_rows,
):
    head = lax.axis_index("head").reshape(1)
    window = lax.axis_index("win").reshape(1)
    weight = jnp.transpose(qkv_weight, (1, 0, 2))
    args = (weight, qkv_bias, norm_gain)
    barrier = lax.optimization_barrier

    mod0 = modulate(latents, modulation)
    sib0 = swap_core(mod0)
    mod1, mod3 = to_y(mod0, -1), to_y(mod0, 1)
    mod2 = to_y(mod0, 2)
    kv_a = project_kv([mod0, sib0], *args, tiles=key_tiles)
    ra1, la1 = along_win(kv_a, 1), along_win(kv_a, -1)
    mod1, mod3, mod2, ra1, la1 = barrier((mod1, mod3, mod2, ra1, la1))
    sib1, sib3, sib2 = swap_core(mod1), swap_core(mod3), swap_core(mod2)
    (half,) = project_others(kv_half_kernel, (mod1, mod3, mod2), *args, (), (3 * ROWS,))
    half, sib1, sib3, sib2 = barrier((half, sib1, sib3, sib2))
    more = ((3 * ROWS, half), (TILE, ra1), (TILE, la1))
    kv_b, right_ac, left_ac = project_others(kv_rest_kernel, (sib1, sib3, sib2), *args, more, (2 * TILE,) * 3)
    rb1, lb1 = along_win(kv_b, 1), along_win(kv_b, -1)
    rac2, lac2 = along_win(right_ac, 1), along_win(left_ac, -1)
    kv_b, w_sent = barrier((kv_b, out_weight))
    w_sib = swap_core(w_sent)
    q = project_q([mod0, sib0, mod1, sib1, mod3, sib3, mod2, sib2], *args)
    hop_args = (head, key_tiles, key_count, q)
    num, den = attend_own(q, (kv_a, kv_b, right_ac))
    rb1, lb1, num, den, w_sib = barrier((rb1, lb1, num, den, w_sib))
    rb2, lb2 = along_win(rb1, 1), along_win(lb1, -1)
    rac3, lac3 = along_win(rac2, 1), along_win(lac2, -1)
    num, den = attend_hop(1, (0, 1), *hop_args, (la1, lb1, lac2), (ra1, rb1, rac2), num, den)
    rb2, lb2, num, den = barrier((rb2, lb2, num, den))
    rb3, lb3 = along_win(rb2, 1), along_win(lb2, -1)
    rc3, lc3 = along_win(rac3[TILE:], 1), along_win(lac3[TILE:], -1)
    num, den = attend_hop(2, (0, 1), *hop_args, (lac2, lb2, lac3), (rac2, rb2, rac3), num, den)
    rb3, lb3, rc3, lc3, num, den = barrier((rb3, lb3, rc3, lc3, num, den))
    right, left = (rac3, rb3, rc3), (lac3, lb3, lc3)
    tiles_prev, tiles_next = (x[TILE : TILE + 1, : 2 * NB].astype(jnp.int32) for x in (ra1, la1))
    last_left, last_right = select_tiles(head, tiles_prev, tiles_next, left, right)
    last_left, last_right = along_win(last_left, -1), along_win(last_right, 1)
    num, den = attend_hop(3, (0, 0), *hop_args, right=right, left=left, num=num, den=den)

    own, sib, edge_a, edge_b = attend_last(head, key_count, q, last_left, last_right, num, den)
    edge_own = lax.ppermute(edge_a, ("win", "head"), strip_pairs(0))
    edge_sib = lax.ppermute(edge_b, ("win", "head"), strip_pairs(1))
    sib = swap_core(sib)
    part = out_own(head, window, strip_rows, own, out_weight)
    part, edge_own, edge_sib, sib = barrier((part, edge_own, edge_sib, sib))
    o0, o1, o3, o2 = out_project(head, window, strip_rows, part, sib, edge_own, edge_sib, out_weight, w_sib)
    total = o0
    for part in (to_y(o1, 1), to_y(o3, -1), to_y(o2, 2)):
        total = total + part.astype(jnp.float32)
    result = latents.astype(jnp.float32) + modulation[2] * (total + out_bias)
    return result.astype(jnp.bfloat16)


def solution(mesh):
    in_specs = (
        P(("win", "head"), None),
        P(),
        P(None, None, "head"),
        P(None, "head"),
        P(),
        P("head", None),
        P(),
        P("win", None),
        P("win"),
        P(),
    )
    out_specs = P(("win", "head"), None)
    return jax.shard_map(shards, mesh=mesh, in_specs=in_specs, out_specs=out_specs, check_vma=False)
```

```python
import functools
import math

import jax
import jax.numpy as jnp
from jax import lax
from jax.experimental import pallas as pl
from jax.experimental.pallas import tpu as pltpu
from jax.sharding import PartitionSpec as P

TILE = 128
TW = 4
NB = 8
OV = 64
ROWS = 64
NOTE = 16
D = 3072
HD = 128
HEADS = 3
LW = HEADS * HD
WINDOWS = 32
GROUPS = 8
MIB = 1 << 20
BIG = 24
COST = pl.CostEstimate(flops=1, bytes_accessed=1, transcendentals=0)
SMEM = functools.partial(pl.BlockSpec, memory_space=pltpu.SMEM)
VMEM = functools.partial(pl.BlockSpec, memory_space=pltpu.VMEM)


def along_win(value, steps):
    return lax.ppermute(value, "win", [(i, (i + steps) % WINDOWS) for i in range(WINDOWS)])


def to_y(value, steps):
    return lax.ppermute(value, "head", [(h, ((h // 2 + steps) % 4) * 2 + h % 2) for h in range(GROUPS)])


def swap_core(value):
    return lax.ppermute(value, "head", [(h, h ^ 1) for h in range(GROUPS)])


def strip_pairs(bottom_core):
    pairs = []
    for w in range(WINDOWS):
        for h in range(GROUPS):
            y, c = h // 2, h % 2
            if c == bottom_core:
                pairs.append((w * GROUPS + h, (w + 1) % WINDOWS * GROUPS + 2 * y))
            else:
                pairs.append((w * GROUPS + h, (w - 1) % WINDOWS * GROUPS + 2 * y + 1))
    return pairs


def modulate_kernel(lat, modulation, out):
    for g in range(ROWS // 16):
        rows = slice(g * 16, (g + 1) * 16)
        wide = lat[rows, :].astype(jnp.float32)
        mean = jnp.sum(wide, axis=-1, keepdims=True) * (1.0 / D)
        centred = wide - mean
        spread = jnp.sum(centred * centred, axis=-1, keepdims=True) * (1.0 / D)
        normed = centred * lax.rsqrt(spread + 1e-06)
        out[rows, :] = ((1.0 + modulation[1:2, :]) * normed + modulation[0:1, :]).astype(jnp.bfloat16)


def modulate(lat, modulation):
    return pl.pallas_call(
        modulate_kernel,
        in_specs=[VMEM()] * 2,
        out_specs=VMEM(),
        out_shape=jax.ShapeDtypeStruct((ROWS, D), jnp.bfloat16),
        compiler_params=pltpu.CompilerParams(vmem_limit_bytes=BIG * MIB),
        cost_estimate=COST,
        name="modulate",
    )(lat, modulation)


def normed_heads(raw, gain):
    out = []
    for h in range(HEADS):
        part = raw[:, h * HD : (h + 1) * HD]
        mean_square = jnp.sum(part * part, axis=-1, keepdims=True) * (1.0 / HD)
        out.append((part * lax.rsqrt(mean_square + 1e-06) * gain).astype(jnp.bfloat16))
    return out


def kv_kernel(parts, carried, *refs):
    weight, bias, gain = refs[parts : parts + 3]
    extra = carried or 1
    carry = refs[parts + 3 : parts + 3 + extra]
    outs, mod_ref = refs[parts + 3 + extra : -1], refs[-1]
    step = pl.program_id(0)
    split = parts * ROWS - (TILE if carried else 0)

    def store(part, cols):
        outs[0][:split, cols] = part[:split]
        for out in outs[1:]:
            out[TILE:, cols] = part[split:]

    @pl.when(step == 0)
    def _():
        for i in range(parts):
            mod_ref[i * ROWS : (i + 1) * ROWS, :] = refs[i][...]
        for ref, out in zip(carry, outs[1:]):
            out[0:TILE, :] = ref[...]
        if not carried:
            lane = lax.broadcasted_iota(jnp.int32, (NOTE, 2 * LW), 1)
            row = jnp.zeros((NOTE, 2 * LW), jnp.int32)
            for e in range(2 * NB):
                row = jnp.where(lane == e, carry[0][0, e], row)
            outs[0][split:, :] = row.astype(jnp.float32).astype(jnp.bfloat16)
        raw = jnp.dot(mod_ref[...], weight[0], preferred_element_type=jnp.float32)
        for h, part in enumerate(normed_heads(raw + bias[1:2, :], gain[1:2, :])):
            store(part, slice(h * HD, (h + 1) * HD))

    @pl.when(step == 1)
    def _():
        raw = jnp.dot(mod_ref[...], weight[0], preferred_element_type=jnp.float32)
        store((raw + bias[2:3, :]).astype(jnp.bfloat16), slice(LW, 2 * LW))


def kv_both(step, rows, weight, bias, gain, store):
    @pl.when(step == 0)
    def _():
        raw = jnp.dot(rows[...], weight[0], preferred_element_type=jnp.float32)
        for h, part in enumerate(normed_heads(raw + bias[1:2, :], gain[1:2, :])):
            store(part, slice(h * HD, (h + 1) * HD))

    @pl.when(step == 1)
    def _():
        raw = jnp.dot(rows[...], weight[0], preferred_element_type=jnp.float32)
        store((raw + bias[2:3, :]).astype(jnp.bfloat16), slice(LW, 2 * LW))


def join_rows(dst, parts):
    for i, part in enumerate(parts):
        dst[i * ROWS : (i + 1) * ROWS, :] = part[...]


def kv_half_kernel(m1, m3, m2, weight, bias, gain, out, rows):
    step = pl.program_id(0)

    @pl.when(step == 0)
    def _():
        join_rows(rows, (m1, m3, m2))

    def store(part, cols):
        out[:, cols] = part

    kv_both(step, rows, weight, bias, gain, store)


def kv_rest_kernel(m1, m3, m2, weight, bias, gain, half, ra, la, kv_b, right, left, rows):
    step = pl.program_id(0)

    def place(values, at, cols):
        kv_b[at : at + ROWS, cols] = values[0:ROWS]
        kv_b[TILE + at : TILE + at + ROWS, cols] = values[ROWS : 2 * ROWS]
        for out in (right, left):
            out[TILE + at : TILE + at + ROWS, cols] = values[2 * ROWS :]

    @pl.when(step == 0)
    def _():
        join_rows(rows, (m1, m3, m2))
        right[0:TILE, :] = ra[...]
        left[0:TILE, :] = la[...]
        place(half[...], 0, slice(0, 2 * LW))

    kv_both(step, rows, weight, bias, gain, lambda part, cols: place(part, ROWS, cols))


def project_others(kernel, mod, weight, bias, gain, more, out_rows):
    whole = lambda shape: pl.BlockSpec(shape, lambda c: (0,) * len(shape))
    return pl.pallas_call(
        kernel,
        grid=(2,),
        in_specs=[whole((ROWS, D))] * 3
        + [pl.BlockSpec((1, D, LW), lambda c: (1 + c, 0, 0)), whole((3, LW)), whole((2, HD))]
        + [whole((n, 2 * LW)) for n, _ in more],
        out_specs=[whole((n, 2 * LW)) for n in out_rows],
        out_shape=[jax.ShapeDtypeStruct((n, 2 * LW), jnp.bfloat16) for n in out_rows],
        scratch_shapes=[pltpu.VMEM((3 * ROWS, D), jnp.bfloat16)],
        compiler_params=pltpu.CompilerParams(vmem_limit_bytes=BIG * MIB),
        cost_estimate=COST,
        name="project_others",
    )(*mod, weight, bias, gain, *(array for _, array in more))


def q_kernel(parts, *refs):
    weight, bias, gain, q_ref, mod_ref = refs[parts:]
    for i in range(parts):
        mod_ref[i * ROWS : (i + 1) * ROWS, :] = refs[i][...]
    raw = jnp.dot(mod_ref[...], weight[0], preferred_element_type=jnp.float32)
    for h, part in enumerate(normed_heads(raw + bias[0:1, :], gain[0:1, :])):
        q_ref[:, h * HD : (h + 1) * HD] = part


def project(kernel, first, count, mod, weight, bias, gain, carry=(), tiles=None):
    parts = len(mod)
    rows = parts * ROWS
    out_rows = [rows - TILE] + [2 * TILE] * len(carry) if carry else [rows + (NOTE if tiles is not None else 0)]
    noted = [tiles] if tiles is not None else []
    whole = lambda shape: pl.BlockSpec(shape, lambda c: (0,) * len(shape))
    out = pl.pallas_call(
        kernel,
        grid=(count,),
        in_specs=[whole((ROWS, D))] * parts
        + [pl.BlockSpec((1, D, LW), lambda c: (first + c, 0, 0)), whole((3, LW)), whole((2, HD))]
        + [whole((TILE, 2 * LW))] * len(carry)
        + [SMEM()] * len(noted),
        out_specs=[whole((n, count * LW)) for n in out_rows],
        out_shape=[jax.ShapeDtypeStruct((n, count * LW), jnp.bfloat16) for n in out_rows],
        scratch_shapes=[pltpu.VMEM((rows, D), jnp.bfloat16)],
        compiler_params=pltpu.CompilerParams(vmem_limit_bytes=BIG * MIB),
        cost_estimate=COST,
        name="project",
    )(*mod, weight, bias, gain, *carry, *noted)
    return out if carry else out[0]


def project_kv(mod, *args, carry=(), tiles=None):
    return project(functools.partial(kv_kernel, len(mod), len(carry)), 1, 2, mod, *args, carry=carry, tiles=tiles)


def project_q(mod, *args):
    return project(functools.partial(q_kernel, len(mod)), 0, 1, mod, *args)


def pick_tile(dst, row, chunks, place):
    a, b, c = chunks

    @pl.when(place == 0)
    def _():
        dst[row : row + TILE, :] = a[...]

    @pl.when(jnp.logical_or(place == 1, place == 2))
    def _():
        dst[row : row + TILE, :] = b[pl.ds(pl.multiple_of((place - 1) * TILE, TILE), TILE), :]

    @pl.when(place == 3)
    def _():
        dst[row : row + TILE, :] = c[...]


def place_of(tile, head):
    step = ((tile & 3) - (head >> 1)) & 3
    return step ^ (step >> 1)


def select_kernel(head, want_left, want_right, la, lb, lc, ra, rb, rc, left, right):
    for k in range(2):
        pick_tile(left, k * TILE, (la, lb, lc), place_of(want_left[0, 12 + k], head[0]))
        pick_tile(right, k * TILE, (ra, rb, rc), place_of(want_right[0, 14 + k], head[0]))


def select_tiles(head, want_left, want_right, left, right):
    return pl.pallas_call(
        select_kernel,
        grid=(1,),
        in_specs=[SMEM()] * 3 + chunk_specs((0, 0)) * 2,
        out_specs=[whole_spec((2 * TILE, 2 * LW))] * 2,
        out_shape=[jax.ShapeDtypeStruct((2 * TILE, 2 * LW), jnp.bfloat16)] * 2,
        compiler_params=pltpu.CompilerParams(vmem_limit_bytes=BIG * MIB),
        cost_estimate=COST,
        name="select_tiles",
    )(head, want_left, want_right, *left, *right)


def accumulate(kv, q_block, live, num, den, first):
    scale = HD**-0.5 * math.log2(math.e)
    for h in range(HEADS):
        cols = slice(h * HD, (h + 1) * HD)
        scores = lax.dot_general(
            q_block(cols), kv[:, cols], (((1,), (1,)), ((), ())), preferred_element_type=jnp.float32
        )
        weights = jnp.exp2(scores * scale)
        parts = []
        for t in range(weights.shape[1] // TILE):
            w = weights[:, t * TILE : (t + 1) * TILE]
            if live is not None:
                w = jnp.where(live(t), w, 0.0)
            parts.append(w)
        total = functools.reduce(jnp.add, parts)
        rounded = jnp.concatenate([w.astype(jnp.bfloat16) for w in parts], axis=1)
        mixed = jnp.dot(rounded, kv[:, LW + h * HD : LW + (h + 1) * HD], preferred_element_type=jnp.float32)
        if first:
            num[0][:, cols] = mixed
            den[0][:, cols] = total
        else:
            num[0][:, cols] = num[1][:, cols] + mixed
            den[0][:, cols] = den[1][:, cols] + total


QB = 256


def own_kernel(q, a, b, c, num, den, kbuf):
    @pl.when(pl.program_id(0) == 0)
    def _():
        kbuf[0:TILE, :] = a[...]
        kbuf[TILE : 3 * TILE, :] = b[...]
        kbuf[3 * TILE :, :] = c[...]

    accumulate(kbuf, lambda cols: q[:, cols], None, (num,), (den,), True)


def hop_kernel(base, head, tiles, count, q, la, lb, lc, ra, rb, rc, num_in, den_in, num, den, kbuf):
    @pl.when(pl.program_id(0) == 0)
    def _():
        for k in range(2):
            pick_tile(kbuf, k * TILE, (la, lb, lc), place_of(tiles[0, base + k], head[0]))
            pick_tile(kbuf, (2 + k) * TILE, (ra, rb, rc), place_of(tiles[0, base + 2 + k], head[0]))

    live = lambda t: base + t < count[0]
    accumulate(kbuf, lambda cols: q[:, cols], live, (num, num_in), (den, den_in), False)


def rows_spec(width):
    return pl.BlockSpec((QB, width), lambda i: (i, 0))


def whole_spec(shape):
    return pl.BlockSpec(shape, lambda i: (0,) * len(shape))


ACC = [jax.ShapeDtypeStruct((512, LW), jnp.float32)] * 2
KBUF = [pltpu.VMEM((4 * TILE, 2 * LW), jnp.bfloat16)]


def chunk_specs(halves):
    a, c = halves
    return [
        pl.BlockSpec((TILE, 2 * LW), lambda i: (a, 0)),
        pl.BlockSpec((2 * TILE, 2 * LW), lambda i: (0, 0)),
        pl.BlockSpec((TILE, 2 * LW), lambda i: (c, 0)),
    ]


def attend_own(q, chunks):
    return pl.pallas_call(
        own_kernel,
        grid=(512 // QB,),
        in_specs=[rows_spec(LW)] + chunk_specs((0, 1)),
        out_specs=[rows_spec(LW)] * 2,
        out_shape=ACC,
        scratch_shapes=KBUF,
        compiler_params=pltpu.CompilerParams(vmem_limit_bytes=BIG * MIB),
        cost_estimate=COST,
        name="attend_own",
    )(q, *chunks)


def attend_hop(hop, halves, head, tiles, count, q, left, right, num, den):
    return pl.pallas_call(
        functools.partial(hop_kernel, 4 * (hop - 1)),
        grid=(512 // QB,),
        in_specs=[SMEM()] * 3 + [rows_spec(LW)] + chunk_specs(halves) * 2 + [rows_spec(LW)] * 2,
        out_specs=[rows_spec(LW)] * 2,
        out_shape=ACC,
        scratch_shapes=KBUF,
        compiler_params=pltpu.CompilerParams(vmem_limit_bytes=BIG * MIB),
        cost_estimate=COST,
        name="attend_hop",
    )(head, tiles, count, q, *left, *right, num, den)


def last_kernel(base, head, count, q, left, right, num_in, den_in, own, sib, edge_a, edge_b, kbuf, num, den):
    step = pl.program_id(0)

    @pl.when(step == 0)
    def _():
        kbuf[0 : 2 * TILE, :] = left[...]
        kbuf[2 * TILE :, :] = right[...]

    live = lambda t: base + t < count[0]
    accumulate(kbuf, lambda cols: q[:, cols], live, (num, num_in), (den, den_in), False)
    for h in range(HEADS):
        cols = slice(h * HD, (h + 1) * HD)
        total = jnp.sum(den[:, cols], axis=-1, keepdims=True)
        out = (num[:, cols] / total).astype(jnp.bfloat16)
        for t in range(QB // TILE):
            at = pl.ds(pl.multiple_of(step * (QB // 2) + t * ROWS, ROWS), ROWS)
            own[at, cols] = out[t * TILE : t * TILE + ROWS]
            sib[at, cols] = out[t * TILE + ROWS : (t + 1) * TILE]

    @pl.when(step == 512 // QB - 1)
    def _():
        core = head[0] & 1
        edge_a[...] = sib[pl.ds(pl.multiple_of(place_of(3 * (1 - core), head[0]) * ROWS, ROWS), ROWS), :]
        edge_b[...] = own[pl.ds(pl.multiple_of(place_of(3 * core, head[0]) * ROWS, ROWS), ROWS), :]


def attend_last(head, count, q, left, right, num, den):
    half = jax.ShapeDtypeStruct((256, LW), jnp.bfloat16)
    edge = jax.ShapeDtypeStruct((ROWS, LW), jnp.bfloat16)
    return pl.pallas_call(
        functools.partial(last_kernel, 12),
        grid=(512 // QB,),
        in_specs=[SMEM()] * 2
        + [rows_spec(LW)]
        + [whole_spec((2 * TILE, 2 * LW))] * 2
        + [rows_spec(LW)] * 2,
        out_specs=[whole_spec((256, LW))] * 2 + [whole_spec((ROWS, LW))] * 2,
        out_shape=[half, half, edge, edge],
        scratch_shapes=KBUF + [pltpu.VMEM((QB, LW), jnp.float32)] * 2,
        compiler_params=pltpu.CompilerParams(vmem_limit_bytes=BIG * MIB),
        cost_estimate=COST,
        name="attend_last",
    )(head, count, q, left, right, num, den)


NCOL = 768


def strip_of(head, window, strips):
    core = head[0] & 1
    return place_of(3 * core, head[0]), strips[(window[0] + core + WINDOWS - 1) & (WINDOWS - 1)], 1 - core


def halve_shared(a, rows, place, shared, top):
    a[...] = rows[...]
    row = lax.broadcasted_iota(jnp.int32, (ROWS, 1), 0)
    low = jnp.where(top == 1, 0, OV - shared)
    keep = jnp.where(jnp.logical_and(row >= low, row < low + shared), 0.5, 1.0)
    at = pl.ds(pl.multiple_of(place * ROWS, ROWS), ROWS)
    a[at, :] = (rows[at, :].astype(jnp.float32) * keep).astype(jnp.bfloat16)


dot = functools.partial(jnp.dot, preferred_element_type=jnp.float32)


def out_own_kernel(head, window, strips, own, w_own, part, a_own):
    @pl.when(pl.program_id(0) == 0)
    def _():
        halve_shared(a_own, own, *strip_of(head, window, strips))

    part[...] = dot(a_own[...], w_own[...])


def out_kernel(head, window, strips, part, sib, edge_own, edge_sib, w_own, w_sib, o0, o1, o3, o2, a_sib, e_own, e_sib):
    place, shared, top = strip_of(head, window, strips)

    @pl.when(pl.program_id(0) == 0)
    def _():
        halve_shared(a_sib, sib, place, shared, top)
        i = lax.broadcasted_iota(jnp.int32, (ROWS, ROWS), 0)
        j = lax.broadcasted_iota(jnp.int32, (ROWS, ROWS), 1)
        offset = jnp.where(top == 1, OV - shared, shared - OV)
        shift = jnp.where(j == i + offset, 0.5, 0.0).astype(jnp.bfloat16)
        e_own[...] = dot(shift, edge_own[...]).astype(jnp.bfloat16)
        e_sib[...] = dot(shift, edge_sib[...]).astype(jnp.bfloat16)

    main = part[...] + dot(a_sib[...], w_sib[...])
    extra = dot(e_own[...], w_own[...]) + dot(e_sib[...], w_sib[...])
    for k, ref in enumerate((o0, o1, o3, o2)):
        block = main[k * ROWS : (k + 1) * ROWS]
        ref[...] = (block + jnp.where(place == k, extra, 0.0)).astype(ref.dtype)


def out_cols(rows):
    return pl.BlockSpec((rows, NCOL), lambda i: (0, i))


def out_own(head, window, strips, own, w_own):
    return pl.pallas_call(
        out_own_kernel,
        grid=(D // NCOL,),
        in_specs=[SMEM()] * 3 + [whole_spec((256, LW)), out_cols(LW)],
        out_specs=out_cols(256),
        out_shape=jax.ShapeDtypeStruct((256, D), jnp.float32),
        scratch_shapes=[pltpu.VMEM((256, LW), jnp.bfloat16)],
        compiler_params=pltpu.CompilerParams(vmem_limit_bytes=BIG * MIB),
        cost_estimate=COST,
        name="out_own",
    )(head, window, strips, own, w_own)


def out_project(head, window, strips, part, sib, edge_own, edge_sib, w_own, w_sib):
    sent = jax.ShapeDtypeStruct((ROWS, D), jnp.bfloat16)
    return pl.pallas_call(
        out_kernel,
        grid=(D // NCOL,),
        in_specs=[SMEM()] * 3
        + [out_cols(256), whole_spec((256, LW))]
        + [whole_spec((ROWS, LW))] * 2
        + [out_cols(LW)] * 2,
        out_specs=[out_cols(ROWS)] * 4,
        out_shape=[jax.ShapeDtypeStruct((ROWS, D), jnp.float32), sent, sent, sent],
        scratch_shapes=[pltpu.VMEM((256, LW), jnp.bfloat16)] + [pltpu.VMEM((ROWS, LW), jnp.bfloat16)] * 2,
        compiler_params=pltpu.CompilerParams(vmem_limit_bytes=BIG * MIB),
        cost_estimate=COST,
        name="out_project",
    )(head, window, strips, part, sib, edge_own, edge_sib, w_own, w_sib)


def shards(
    latents,
    modulation,
    qkv_weight,
    qkv_bias,
    norm_gain,
    out_weight,
    out_bias,
    key_tiles,
    key_count,
    strip_rows,
):
    head = lax.axis_index("head").reshape(1)
    window = lax.axis_index("win").reshape(1)
    weight = jnp.transpose(qkv_weight, (1, 0, 2))
    args = (weight, qkv_bias, norm_gain)
    barrier = lax.optimization_barrier

    mod0 = modulate(latents, modulation)
    sib0 = swap_core(mod0)
    mod1, mod3 = to_y(mod0, -1), to_y(mod0, 1)
    mod2 = to_y(mod0, 2)
    kv_a = project_kv([mod0, sib0], *args, tiles=key_tiles)
    ra1, la1 = along_win(kv_a, 1), along_win(kv_a, -1)
    mod1, mod3, mod2, ra1, la1 = barrier((mod1, mod3, mod2, ra1, la1))
    sib1, sib3, sib2 = swap_core(mod1), swap_core(mod3), swap_core(mod2)
    (half,) = project_others(kv_half_kernel, (mod1, mod3, mod2), *args, (), (3 * ROWS,))
    half, sib1, sib3, sib2 = barrier((half, sib1, sib3, sib2))
    more = ((3 * ROWS, half), (TILE, ra1), (TILE, la1))
    kv_b, right_ac, left_ac = project_others(kv_rest_kernel, (sib1, sib3, sib2), *args, more, (2 * TILE,) * 3)
    rb1, lb1 = along_win(kv_b, 1), along_win(kv_b, -1)
    rac2, lac2 = along_win(right_ac, 1), along_win(left_ac, -1)
    kv_b, w_sent = barrier((kv_b, out_weight))
    w_sib = swap_core(w_sent)
    q = project_q([mod0, sib0, mod1, sib1, mod3, sib3, mod2, sib2], *args)
    hop_args = (head, key_tiles, key_count, q)
    num, den = attend_own(q, (kv_a, kv_b, right_ac))
    rb1, lb1, num, den = barrier((rb1, lb1, num, den))
    rb2, lb2 = along_win(rb1, 1), along_win(lb1, -1)
    rac3, lac3 = along_win(rac2, 1), along_win(lac2, -1)
    num, den = attend_hop(1, (0, 1), *hop_args, (la1, lb1, lac2), (ra1, rb1, rac2), num, den)
    rb2, lb2, num, den = barrier((rb2, lb2, num, den))
    rb3, lb3 = along_win(rb2, 1), along_win(lb2, -1)
    rc3, lc3 = along_win(rac3[TILE:], 1), along_win(lac3[TILE:], -1)
    num, den = attend_hop(2, (0, 1), *hop_args, (lac2, lb2, lac3), (rac2, rb2, rac3), num, den)
    rb3, lb3, rc3, lc3, num, den = barrier((rb3, lb3, rc3, lc3, num, den))
    right, left = (rac3, rb3, rc3), (lac3, lb3, lc3)
    tiles_prev, tiles_next = (x[TILE : TILE + 1, : 2 * NB].astype(jnp.int32) for x in (ra1, la1))
    last_left, last_right = select_tiles(head, tiles_prev, tiles_next, left, right)
    last_left, last_right = along_win(last_left, -1), along_win(last_right, 1)
    num, den = attend_hop(3, (0, 0), *hop_args, right=right, left=left, num=num, den=den)

    own, sib, edge_a, edge_b = attend_last(head, key_count, q, last_left, last_right, num, den)
    edge_own = lax.ppermute(edge_a, ("win", "head"), strip_pairs(0))
    edge_sib = lax.ppermute(edge_b, ("win", "head"), strip_pairs(1))
    sib = swap_core(sib)
    part = out_own(head, window, strip_rows, own, out_weight)
    part, edge_own, edge_sib, sib = barrier((part, edge_own, edge_sib, sib))
    o0, o1, o3, o2 = out_project(head, window, strip_rows, part, sib, edge_own, edge_sib, out_weight, w_sib)
    total = o0
    for part in (to_y(o1, 1), to_y(o3, -1), to_y(o2, 2)):
        total = total + part.astype(jnp.float32)
    result = latents.astype(jnp.float32) + modulation[2] * (total + out_bias)
    return result.astype(jnp.bfloat16)


def solution(mesh):
    in_specs = (
        P(("win", "head"), None),
        P(),
        P(None, None, "head"),
        P(None, "head"),
        P(),
        P("head", None),
        P(),
        P("win", None),
        P("win"),
        P(),
    )
    out_specs = P(("win", "head"), None)
    return jax.shard_map(shards, mesh=mesh, in_specs=in_specs, out_specs=out_specs, check_vma=False)
```

```python
import functools
import math

import jax
import jax.numpy as jnp
from jax import lax
from jax.experimental import pallas as pl
from jax.experimental.pallas import tpu as pltpu
from jax.sharding import PartitionSpec as P

TILE = 128
TW = 4
NB = 8
OV = 64
ROWS = 64
NOTE = 16
D = 3072
HD = 128
HEADS = 3
LW = HEADS * HD
WINDOWS = 32
GROUPS = 8
MIB = 1 << 20
BIG = 24
COST = pl.CostEstimate(flops=1, bytes_accessed=1, transcendentals=0)
SMEM = functools.partial(pl.BlockSpec, memory_space=pltpu.SMEM)
VMEM = functools.partial(pl.BlockSpec, memory_space=pltpu.VMEM)


def along_win(value, steps):
    return lax.ppermute(value, "win", [(i, (i + steps) % WINDOWS) for i in range(WINDOWS)])


def to_y(value, steps):
    return lax.ppermute(value, "head", [(h, ((h // 2 + steps) % 4) * 2 + h % 2) for h in range(GROUPS)])


def swap_core(value):
    return lax.ppermute(value, "head", [(h, h ^ 1) for h in range(GROUPS)])


def strip_pairs(bottom_core):
    pairs = []
    for w in range(WINDOWS):
        for h in range(GROUPS):
            y, c = h // 2, h % 2
            if c == bottom_core:
                pairs.append((w * GROUPS + h, (w + 1) % WINDOWS * GROUPS + 2 * y))
            else:
                pairs.append((w * GROUPS + h, (w - 1) % WINDOWS * GROUPS + 2 * y + 1))
    return pairs


def modulate_kernel(lat, modulation, out):
    for g in range(ROWS // 16):
        rows = slice(g * 16, (g + 1) * 16)
        wide = lat[rows, :].astype(jnp.float32)
        mean = jnp.sum(wide, axis=-1, keepdims=True) * (1.0 / D)
        centred = wide - mean
        spread = jnp.sum(centred * centred, axis=-1, keepdims=True) * (1.0 / D)
        normed = centred * lax.rsqrt(spread + 1e-06)
        out[rows, :] = ((1.0 + modulation[1:2, :]) * normed + modulation[0:1, :]).astype(jnp.bfloat16)


def modulate(lat, modulation):
    return pl.pallas_call(
        modulate_kernel,
        in_specs=[VMEM()] * 2,
        out_specs=VMEM(),
        out_shape=jax.ShapeDtypeStruct((ROWS, D), jnp.bfloat16),
        compiler_params=pltpu.CompilerParams(vmem_limit_bytes=BIG * MIB),
        cost_estimate=COST,
        name="modulate",
    )(lat, modulation)


def normed_heads(raw, gain):
    out = []
    for h in range(HEADS):
        part = raw[:, h * HD : (h + 1) * HD]
        mean_square = jnp.sum(part * part, axis=-1, keepdims=True) * (1.0 / HD)
        out.append((part * lax.rsqrt(mean_square + 1e-06) * gain).astype(jnp.bfloat16))
    return out


def kv_kernel(parts, carried, *refs):
    weight, bias, gain = refs[parts : parts + 3]
    extra = carried or 1
    carry = refs[parts + 3 : parts + 3 + extra]
    outs, mod_ref = refs[parts + 3 + extra : -1], refs[-1]
    step = pl.program_id(0)
    split = parts * ROWS - (TILE if carried else 0)

    def store(part, cols):
        outs[0][:split, cols] = part[:split]
        for out in outs[1:]:
            out[TILE:, cols] = part[split:]

    @pl.when(step == 0)
    def _():
        for i in range(parts):
            mod_ref[i * ROWS : (i + 1) * ROWS, :] = refs[i][...]
        for ref, out in zip(carry, outs[1:]):
            out[0:TILE, :] = ref[...]
        if not carried:
            lane = lax.broadcasted_iota(jnp.int32, (NOTE, 2 * LW), 1)
            row = jnp.zeros((NOTE, 2 * LW), jnp.int32)
            for e in range(2 * NB):
                row = jnp.where(lane == e, carry[0][0, e], row)
            outs[0][split:, :] = row.astype(jnp.float32).astype(jnp.bfloat16)
        raw = jnp.dot(mod_ref[...], weight[0], preferred_element_type=jnp.float32)
        for h, part in enumerate(normed_heads(raw + bias[1:2, :], gain[1:2, :])):
            store(part, slice(h * HD, (h + 1) * HD))

    @pl.when(step == 1)
    def _():
        raw = jnp.dot(mod_ref[...], weight[0], preferred_element_type=jnp.float32)
        store((raw + bias[2:3, :]).astype(jnp.bfloat16), slice(LW, 2 * LW))


def kv_both(step, rows, weight, bias, gain, store):
    @pl.when(step == 0)
    def _():
        raw = jnp.dot(rows[...], weight[0], preferred_element_type=jnp.float32)
        for h, part in enumerate(normed_heads(raw + bias[1:2, :], gain[1:2, :])):
            store(part, slice(h * HD, (h + 1) * HD))

    @pl.when(step == 1)
    def _():
        raw = jnp.dot(rows[...], weight[0], preferred_element_type=jnp.float32)
        store((raw + bias[2:3, :]).astype(jnp.bfloat16), slice(LW, 2 * LW))


def join_rows(dst, parts):
    for i, part in enumerate(parts):
        dst[i * ROWS : (i + 1) * ROWS, :] = part[...]


def kv_half_kernel(m1, m3, m2, weight, bias, gain, out, rows):
    step = pl.program_id(0)

    @pl.when(step == 0)
    def _():
        join_rows(rows, (m1, m3, m2))

    def store(part, cols):
        out[:, cols] = part

    kv_both(step, rows, weight, bias, gain, store)


def kv_rest_kernel(m1, m3, m2, weight, bias, gain, half, ra, la, kv_b, right, left, rows):
    step = pl.program_id(0)

    def place(values, at, cols):
        kv_b[at : at + ROWS, cols] = values[0:ROWS]
        kv_b[TILE + at : TILE + at + ROWS, cols] = values[ROWS : 2 * ROWS]
        for out in (right, left):
            out[TILE + at : TILE + at + ROWS, cols] = values[2 * ROWS :]

    @pl.when(step == 0)
    def _():
        join_rows(rows, (m1, m3, m2))
        right[0:TILE, :] = ra[...]
        left[0:TILE, :] = la[...]
        place(half[...], 0, slice(0, 2 * LW))

    kv_both(step, rows, weight, bias, gain, lambda part, cols: place(part, ROWS, cols))


def project_others(kernel, mod, weight, bias, gain, more, out_rows):
    whole = lambda shape: pl.BlockSpec(shape, lambda c: (0,) * len(shape))
    return pl.pallas_call(
        kernel,
        grid=(2,),
        in_specs=[whole((ROWS, D))] * 3
        + [pl.BlockSpec((1, D, LW), lambda c: (1 + c, 0, 0)), whole((3, LW)), whole((2, HD))]
        + [whole((n, 2 * LW)) for n, _ in more],
        out_specs=[whole((n, 2 * LW)) for n in out_rows],
        out_shape=[jax.ShapeDtypeStruct((n, 2 * LW), jnp.bfloat16) for n in out_rows],
        scratch_shapes=[pltpu.VMEM((3 * ROWS, D), jnp.bfloat16)],
        compiler_params=pltpu.CompilerParams(vmem_limit_bytes=BIG * MIB),
        cost_estimate=COST,
        name="project_others",
    )(*mod, weight, bias, gain, *(array for _, array in more))


def q_kernel(parts, *refs):
    weight, bias, gain, q_ref, mod_ref = refs[parts:]
    for i in range(parts):
        mod_ref[i * ROWS : (i + 1) * ROWS, :] = refs[i][...]
    raw = jnp.dot(mod_ref[...], weight[0], preferred_element_type=jnp.float32)
    for h, part in enumerate(normed_heads(raw + bias[0:1, :], gain[0:1, :])):
        q_ref[:, h * HD : (h + 1) * HD] = part


def project(kernel, first, count, mod, weight, bias, gain, carry=(), tiles=None):
    parts = len(mod)
    rows = parts * ROWS
    out_rows = [rows - TILE] + [2 * TILE] * len(carry) if carry else [rows + (NOTE if tiles is not None else 0)]
    noted = [tiles] if tiles is not None else []
    whole = lambda shape: pl.BlockSpec(shape, lambda c: (0,) * len(shape))
    out = pl.pallas_call(
        kernel,
        grid=(count,),
        in_specs=[whole((ROWS, D))] * parts
        + [pl.BlockSpec((1, D, LW), lambda c: (first + c, 0, 0)), whole((3, LW)), whole((2, HD))]
        + [whole((TILE, 2 * LW))] * len(carry)
        + [SMEM()] * len(noted),
        out_specs=[whole((n, count * LW)) for n in out_rows],
        out_shape=[jax.ShapeDtypeStruct((n, count * LW), jnp.bfloat16) for n in out_rows],
        scratch_shapes=[pltpu.VMEM((rows, D), jnp.bfloat16)],
        compiler_params=pltpu.CompilerParams(vmem_limit_bytes=BIG * MIB),
        cost_estimate=COST,
        name="project",
    )(*mod, weight, bias, gain, *carry, *noted)
    return out if carry else out[0]


def project_kv(mod, *args, carry=(), tiles=None):
    return project(functools.partial(kv_kernel, len(mod), len(carry)), 1, 2, mod, *args, carry=carry, tiles=tiles)


def project_q(mod, *args):
    return project(functools.partial(q_kernel, len(mod)), 0, 1, mod, *args)


def pick_tile(dst, row, chunks, place):
    a, b, c = chunks

    @pl.when(place == 0)
    def _():
        dst[row : row + TILE, :] = a[...]

    @pl.when(jnp.logical_or(place == 1, place == 2))
    def _():
        dst[row : row + TILE, :] = b[pl.ds(pl.multiple_of((place - 1) * TILE, TILE), TILE), :]

    @pl.when(place == 3)
    def _():
        dst[row : row + TILE, :] = c[...]


def place_of(tile, head):
    step = ((tile & 3) - (head >> 1)) & 3
    return step ^ (step >> 1)


def select_kernel(head, want_left, want_right, la, lb, lc, ra, rb, rc, left, right):
    for k in range(2):
        pick_tile(left, k * TILE, (la, lb, lc), place_of(want_left[0, 12 + k], head[0]))
        pick_tile(right, k * TILE, (ra, rb, rc), place_of(want_right[0, 14 + k], head[0]))


def select_tiles(head, want_left, want_right, left, right):
    return pl.pallas_call(
        select_kernel,
        grid=(1,),
        in_specs=[SMEM()] * 3 + chunk_specs((0, 0)) * 2,
        out_specs=[whole_spec((2 * TILE, 2 * LW))] * 2,
        out_shape=[jax.ShapeDtypeStruct((2 * TILE, 2 * LW), jnp.bfloat16)] * 2,
        compiler_params=pltpu.CompilerParams(vmem_limit_bytes=BIG * MIB),
        cost_estimate=COST,
        name="select_tiles",
    )(head, want_left, want_right, *left, *right)


def accumulate(kv, q_block, live, num, den, first):
    scale = HD**-0.5 * math.log2(math.e)
    for h in range(HEADS):
        cols = slice(h * HD, (h + 1) * HD)
        scores = lax.dot_general(
            q_block(cols), kv[:, cols], (((1,), (1,)), ((), ())), preferred_element_type=jnp.float32
        )
        weights = jnp.exp2(scores * scale)
        parts = []
        for t in range(weights.shape[1] // TILE):
            w = weights[:, t * TILE : (t + 1) * TILE]
            if live is not None:
                w = jnp.where(live(t), w, 0.0)
            parts.append(w)
        total = functools.reduce(jnp.add, parts)
        rounded = jnp.concatenate([w.astype(jnp.bfloat16) for w in parts], axis=1)
        mixed = jnp.dot(rounded, kv[:, LW + h * HD : LW + (h + 1) * HD], preferred_element_type=jnp.float32)
        if first:
            num[0][:, cols] = mixed
            den[0][:, cols] = total
        else:
            num[0][:, cols] = num[1][:, cols] + mixed
            den[0][:, cols] = den[1][:, cols] + total


QB = 256


def own_kernel(q, a, b, c, num, den, kbuf):
    @pl.when(pl.program_id(0) == 0)
    def _():
        kbuf[0:TILE, :] = a[...]
        kbuf[TILE : 3 * TILE, :] = b[...]
        kbuf[3 * TILE :, :] = c[...]

    accumulate(kbuf, lambda cols: q[:, cols], None, (num,), (den,), True)


def hop_kernel(base, head, tiles, count, q, la, lb, lc, ra, rb, rc, num_in, den_in, num, den, kbuf):
    @pl.when(pl.program_id(0) == 0)
    def _():
        for k in range(2):
            pick_tile(kbuf, k * TILE, (la, lb, lc), place_of(tiles[0, base + k], head[0]))
            pick_tile(kbuf, (2 + k) * TILE, (ra, rb, rc), place_of(tiles[0, base + 2 + k], head[0]))

    live = lambda t: base + t < count[0]
    accumulate(kbuf, lambda cols: q[:, cols], live, (num, num_in), (den, den_in), False)


def rows_spec(width):
    return pl.BlockSpec((QB, width), lambda i: (i, 0))


def whole_spec(shape):
    return pl.BlockSpec(shape, lambda i: (0,) * len(shape))


ACC = [jax.ShapeDtypeStruct((512, LW), jnp.float32)] * 2
KBUF = [pltpu.VMEM((4 * TILE, 2 * LW), jnp.bfloat16)]


def chunk_specs(halves):
    a, c = halves
    return [
        pl.BlockSpec((TILE, 2 * LW), lambda i: (a, 0)),
        pl.BlockSpec((2 * TILE, 2 * LW), lambda i: (0, 0)),
        pl.BlockSpec((TILE, 2 * LW), lambda i: (c, 0)),
    ]


def attend_own(q, chunks):
    return pl.pallas_call(
        own_kernel,
        grid=(512 // QB,),
        in_specs=[rows_spec(LW)] + chunk_specs((0, 1)),
        out_specs=[rows_spec(LW)] * 2,
        out_shape=ACC,
        scratch_shapes=KBUF,
        compiler_params=pltpu.CompilerParams(vmem_limit_bytes=BIG * MIB),
        cost_estimate=COST,
        name="attend_own",
    )(q, *chunks)


def attend_hop(hop, halves, head, tiles, count, q, left, right, num, den):
    return pl.pallas_call(
        functools.partial(hop_kernel, 4 * (hop - 1)),
        grid=(512 // QB,),
        in_specs=[SMEM()] * 3 + [rows_spec(LW)] + chunk_specs(halves) * 2 + [rows_spec(LW)] * 2,
        out_specs=[rows_spec(LW)] * 2,
        out_shape=ACC,
        scratch_shapes=KBUF,
        compiler_params=pltpu.CompilerParams(vmem_limit_bytes=BIG * MIB),
        cost_estimate=COST,
        name="attend_hop",
    )(head, tiles, count, q, *left, *right, num, den)


def last_kernel(base, head, count, q, left, right, num_in, den_in, own, sib, edge_a, edge_b, kbuf, num, den):
    step = pl.program_id(0)

    @pl.when(step == 0)
    def _():
        kbuf[0 : 2 * TILE, :] = left[...]
        kbuf[2 * TILE :, :] = right[...]

    live = lambda t: base + t < count[0]
    accumulate(kbuf, lambda cols: q[:, cols], live, (num, num_in), (den, den_in), False)
    for h in range(HEADS):
        cols = slice(h * HD, (h + 1) * HD)
        total = jnp.sum(den[:, cols], axis=-1, keepdims=True)
        out = (num[:, cols] / total).astype(jnp.bfloat16)
        for t in range(QB // TILE):
            at = pl.ds(pl.multiple_of(step * (QB // 2) + t * ROWS, ROWS), ROWS)
            own[at, cols] = out[t * TILE : t * TILE + ROWS]
            sib[at, cols] = out[t * TILE + ROWS : (t + 1) * TILE]

    @pl.when(step == 512 // QB - 1)
    def _():
        core = head[0] & 1
        edge_a[...] = sib[pl.ds(pl.multiple_of(place_of(3 * (1 - core), head[0]) * ROWS, ROWS), ROWS), :]
        edge_b[...] = own[pl.ds(pl.multiple_of(place_of(3 * core, head[0]) * ROWS, ROWS), ROWS), :]


def attend_last(head, count, q, left, right, num, den):
    half = jax.ShapeDtypeStruct((256, LW), jnp.bfloat16)
    edge = jax.ShapeDtypeStruct((ROWS, LW), jnp.bfloat16)
    return pl.pallas_call(
        functools.partial(last_kernel, 12),
        grid=(512 // QB,),
        in_specs=[SMEM()] * 2
        + [rows_spec(LW)]
        + [whole_spec((2 * TILE, 2 * LW))] * 2
        + [rows_spec(LW)] * 2,
        out_specs=[whole_spec((256, LW))] * 2 + [whole_spec((ROWS, LW))] * 2,
        out_shape=[half, half, edge, edge],
        scratch_shapes=KBUF + [pltpu.VMEM((QB, LW), jnp.float32)] * 2,
        compiler_params=pltpu.CompilerParams(vmem_limit_bytes=BIG * MIB),
        cost_estimate=COST,
        name="attend_last",
    )(head, count, q, left, right, num, den)


NCOL = 768


def strip_of(head, window, strips):
    core = head[0] & 1
    return place_of(3 * core, head[0]), strips[(window[0] + core + WINDOWS - 1) & (WINDOWS - 1)], 1 - core


def halve_shared(a, rows, place, shared, top):
    a[...] = rows[...]
    row = lax.broadcasted_iota(jnp.int32, (ROWS, 1), 0)
    low = jnp.where(top == 1, 0, OV - shared)
    keep = jnp.where(jnp.logical_and(row >= low, row < low + shared), 0.5, 1.0)
    at = pl.ds(pl.multiple_of(place * ROWS, ROWS), ROWS)
    a[at, :] = (rows[at, :].astype(jnp.float32) * keep).astype(jnp.bfloat16)


dot = functools.partial(jnp.dot, preferred_element_type=jnp.float32)


def out_own_kernel(head, window, strips, own, w_own, part, a_own):
    @pl.when(pl.program_id(0) == 0)
    def _():
        halve_shared(a_own, own, *strip_of(head, window, strips))

    part[...] = dot(a_own[...], w_own[...])


def out_kernel(head, window, strips, part, sib, edge_own, edge_sib, w_own, w_sib, o0, o1, o3, o2, a_sib, e_own, e_sib):
    place, shared, top = strip_of(head, window, strips)

    @pl.when(pl.program_id(0) == 0)
    def _():
        halve_shared(a_sib, sib, place, shared, top)
        i = lax.broadcasted_iota(jnp.int32, (ROWS, ROWS), 0)
        j = lax.broadcasted_iota(jnp.int32, (ROWS, ROWS), 1)
        offset = jnp.where(top == 1, OV - shared, shared - OV)
        shift = jnp.where(j == i + offset, 0.5, 0.0).astype(jnp.bfloat16)
        e_own[...] = dot(shift, edge_own[...]).astype(jnp.bfloat16)
        e_sib[...] = dot(shift, edge_sib[...]).astype(jnp.bfloat16)

    main = part[...] + dot(a_sib[...], w_sib[...])
    extra = dot(e_own[...], w_own[...]) + dot(e_sib[...], w_sib[...])
    for k, ref in enumerate((o0, o1, o3, o2)):
        block = main[k * ROWS : (k + 1) * ROWS]
        ref[...] = (block + jnp.where(place == k, extra, 0.0)).astype(ref.dtype)


def out_cols(rows):
    return pl.BlockSpec((rows, NCOL), lambda i: (0, i))


def out_own(head, window, strips, own, w_own):
    return pl.pallas_call(
        out_own_kernel,
        grid=(D // NCOL,),
        in_specs=[SMEM()] * 3 + [whole_spec((256, LW)), out_cols(LW)],
        out_specs=out_cols(256),
        out_shape=jax.ShapeDtypeStruct((256, D), jnp.float32),
        scratch_shapes=[pltpu.VMEM((256, LW), jnp.bfloat16)],
        compiler_params=pltpu.CompilerParams(vmem_limit_bytes=BIG * MIB),
        cost_estimate=COST,
        name="out_own",
    )(head, window, strips, own, w_own)


def out_project(head, window, strips, part, sib, edge_own, edge_sib, w_own, w_sib):
    sent = jax.ShapeDtypeStruct((ROWS, D), jnp.bfloat16)
    return pl.pallas_call(
        out_kernel,
        grid=(D // NCOL,),
        in_specs=[SMEM()] * 3
        + [out_cols(256), whole_spec((256, LW))]
        + [whole_spec((ROWS, LW))] * 2
        + [out_cols(LW)] * 2,
        out_specs=[out_cols(ROWS)] * 4,
        out_shape=[jax.ShapeDtypeStruct((ROWS, D), jnp.float32), sent, sent, sent],
        scratch_shapes=[pltpu.VMEM((256, LW), jnp.bfloat16)] + [pltpu.VMEM((ROWS, LW), jnp.bfloat16)] * 2,
        compiler_params=pltpu.CompilerParams(vmem_limit_bytes=BIG * MIB),
        cost_estimate=COST,
        name="out_project",
    )(head, window, strips, part, sib, edge_own, edge_sib, w_own, w_sib)


def shards(
    latents,
    modulation,
    qkv_weight,
    qkv_bias,
    norm_gain,
    out_weight,
    out_bias,
    key_tiles,
    key_count,
    strip_rows,
):
    head = lax.axis_index("head").reshape(1)
    window = lax.axis_index("win").reshape(1)
    weight = jnp.transpose(qkv_weight, (1, 0, 2))
    args = (weight, qkv_bias, norm_gain)
    barrier = lax.optimization_barrier

    mod0 = modulate(latents, modulation)
    sib0 = swap_core(mod0)
    mod1, mod3 = to_y(mod0, -1), to_y(mod0, 1)
    mod2 = to_y(mod0, 2)
    kv_a = project_kv([mod0, sib0], *args, tiles=key_tiles)
    ra1, la1 = along_win(kv_a, 1), along_win(kv_a, -1)
    mod1, mod3, mod2, ra1, la1 = barrier((mod1, mod3, mod2, ra1, la1))
    sib1, sib3, sib2 = swap_core(mod1), swap_core(mod3), swap_core(mod2)
    (half,) = project_others(kv_half_kernel, (mod1, mod3, mod2), *args, (), (3 * ROWS,))
    half, sib1, sib3, sib2 = barrier((half, sib1, sib3, sib2))
    more = ((3 * ROWS, half), (TILE, ra1), (TILE, la1))
    kv_b, right_ac, left_ac = project_others(kv_rest_kernel, (sib1, sib3, sib2), *args, more, (2 * TILE,) * 3)
    rb1, lb1 = along_win(kv_b, 1), along_win(kv_b, -1)
    rac2, lac2 = along_win(right_ac, 1), along_win(left_ac, -1)
    kv_b, w_sent = barrier((kv_b, out_weight))
    w_sib = swap_core(w_sent)
    q = project_q([mod0, sib0, mod1, sib1, mod3, sib3, mod2, sib2], *args)
    hop_args = (head, key_tiles, key_count, q)
    num, den = attend_own(q, (kv_a, kv_b, right_ac))
    rb1, lb1, num, den, w_sib = barrier((rb1, lb1, num, den, w_sib))
    rb2, lb2 = along_win(rb1, 1), along_win(lb1, -1)
    rac3, lac3 = along_win(rac2, 1), along_win(lac2, -1)
    rb2, lb2, num, den = barrier((rb2, lb2, num, den))
    rb3, lb3 = along_win(rb2, 1), along_win(lb2, -1)
    num, den = attend_hop(1, (0, 1), *hop_args, (la1, lb1, lac2), (ra1, rb1, rac2), num, den)
    rac3, lac3, num, den = barrier((rac3, lac3, num, den))
    rc3, lc3 = along_win(rac3[TILE:], 1), along_win(lac3[TILE:], -1)
    num, den = attend_hop(2, (0, 1), *hop_args, (lac2, lb2, lac3), (rac2, rb2, rac3), num, den)
    rb3, lb3, rc3, lc3, num, den = barrier((rb3, lb3, rc3, lc3, num, den))
    right, left = (rac3, rb3, rc3), (lac3, lb3, lc3)
    tiles_prev, tiles_next = (x[TILE : TILE + 1, : 2 * NB].astype(jnp.int32) for x in (ra1, la1))
    last_left, last_right = select_tiles(head, tiles_prev, tiles_next, left, right)
    last_left, last_right = along_win(last_left, -1), along_win(last_right, 1)
    num, den = attend_hop(3, (0, 0), *hop_args, right=right, left=left, num=num, den=den)

    own, sib, edge_a, edge_b = attend_last(head, key_count, q, last_left, last_right, num, den)
    edge_own = lax.ppermute(edge_a, ("win", "head"), strip_pairs(0))
    edge_sib = lax.ppermute(edge_b, ("win", "head"), strip_pairs(1))
    sib = swap_core(sib)
    part = out_own(head, window, strip_rows, own, out_weight)
    part, edge_own, edge_sib, sib = barrier((part, edge_own, edge_sib, sib))
    o0, o1, o3, o2 = out_project(head, window, strip_rows, part, sib, edge_own, edge_sib, out_weight, w_sib)
    total = o0
    for part in (to_y(o1, 1), to_y(o3, -1), to_y(o2, 2)):
        total = total + part.astype(jnp.float32)
    result = latents.astype(jnp.float32) + modulation[2] * (total + out_bias)
    return result.astype(jnp.bfloat16)


def solution(mesh):
    in_specs = (
        P(("win", "head"), None),
        P(),
        P(None, None, "head"),
        P(None, "head"),
        P(),
        P("head", None),
        P(),
        P("win", None),
        P("win"),
        P(),
    )
    out_specs = P(("win", "head"), None)
    return jax.shard_map(shards, mesh=mesh, in_specs=in_specs, out_specs=out_specs, check_vma=False)
```

```python
import functools
import math

import jax
import jax.numpy as jnp
from jax import lax
from jax.experimental import pallas as pl
from jax.experimental.pallas import tpu as pltpu
from jax.sharding import PartitionSpec as P

TILE = 128
TW = 4
NB = 8
OV = 64
ROWS = 64
NOTE = 16
D = 3072
HD = 128
HEADS = 3
LW = HEADS * HD
WINDOWS = 32
GROUPS = 8
MIB = 1 << 20
BIG = 24
COST = pl.CostEstimate(flops=1, bytes_accessed=1, transcendentals=0)
SMEM = functools.partial(pl.BlockSpec, memory_space=pltpu.SMEM)
VMEM = functools.partial(pl.BlockSpec, memory_space=pltpu.VMEM)


def along_win(value, steps):
    return lax.ppermute(value, "win", [(i, (i + steps) % WINDOWS) for i in range(WINDOWS)])


def to_y(value, steps):
    return lax.ppermute(value, "head", [(h, ((h // 2 + steps) % 4) * 2 + h % 2) for h in range(GROUPS)])


def swap_core(value):
    return lax.ppermute(value, "head", [(h, h ^ 1) for h in range(GROUPS)])


def strip_pairs(bottom_core):
    pairs = []
    for w in range(WINDOWS):
        for h in range(GROUPS):
            y, c = h // 2, h % 2
            if c == bottom_core:
                pairs.append((w * GROUPS + h, (w + 1) % WINDOWS * GROUPS + 2 * y))
            else:
                pairs.append((w * GROUPS + h, (w - 1) % WINDOWS * GROUPS + 2 * y + 1))
    return pairs


def modulate_kernel(lat, modulation, out):
    for g in range(ROWS // 16):
        rows = slice(g * 16, (g + 1) * 16)
        wide = lat[rows, :].astype(jnp.float32)
        mean = jnp.sum(wide, axis=-1, keepdims=True) * (1.0 / D)
        centred = wide - mean
        spread = jnp.sum(centred * centred, axis=-1, keepdims=True) * (1.0 / D)
        normed = centred * lax.rsqrt(spread + 1e-06)
        out[rows, :] = ((1.0 + modulation[1:2, :]) * normed + modulation[0:1, :]).astype(jnp.bfloat16)


def modulate(lat, modulation):
    return pl.pallas_call(
        modulate_kernel,
        in_specs=[VMEM()] * 2,
        out_specs=VMEM(),
        out_shape=jax.ShapeDtypeStruct((ROWS, D), jnp.bfloat16),
        compiler_params=pltpu.CompilerParams(vmem_limit_bytes=BIG * MIB),
        cost_estimate=COST,
        name="modulate",
    )(lat, modulation)


def normed_heads(raw, gain):
    out = []
    for h in range(HEADS):
        part = raw[:, h * HD : (h + 1) * HD]
        mean_square = jnp.sum(part * part, axis=-1, keepdims=True) * (1.0 / HD)
        out.append((part * lax.rsqrt(mean_square + 1e-06) * gain).astype(jnp.bfloat16))
    return out


def kv_kernel(parts, carried, *refs):
    weight, bias, gain = refs[parts : parts + 3]
    extra = carried or 1
    carry = refs[parts + 3 : parts + 3 + extra]
    outs, mod_ref = refs[parts + 3 + extra : -1], refs[-1]
    step = pl.program_id(0)
    split = parts * ROWS - (TILE if carried else 0)

    def store(part, cols):
        outs[0][:split, cols] = part[:split]
        for out in outs[1:]:
            out[TILE:, cols] = part[split:]

    @pl.when(step == 0)
    def _():
        for i in range(parts):
            mod_ref[i * ROWS : (i + 1) * ROWS, :] = refs[i][...]
        for ref, out in zip(carry, outs[1:]):
            out[0:TILE, :] = ref[...]
        if not carried:
            lane = lax.broadcasted_iota(jnp.int32, (NOTE, 2 * LW), 1)
            row = jnp.zeros((NOTE, 2 * LW), jnp.int32)
            for e in range(2 * NB):
                row = jnp.where(lane == e, carry[0][0, e], row)
            outs[0][split:, :] = row.astype(jnp.float32).astype(jnp.bfloat16)
        raw = jnp.dot(mod_ref[...], weight[0], preferred_element_type=jnp.float32)
        for h, part in enumerate(normed_heads(raw + bias[1:2, :], gain[1:2, :])):
            store(part, slice(h * HD, (h + 1) * HD))

    @pl.when(step == 1)
    def _():
        raw = jnp.dot(mod_ref[...], weight[0], preferred_element_type=jnp.float32)
        store((raw + bias[2:3, :]).astype(jnp.bfloat16), slice(LW, 2 * LW))


def kv_both(step, rows, weight, bias, gain, store):
    @pl.when(step == 0)
    def _():
        raw = jnp.dot(rows[...], weight[0], preferred_element_type=jnp.float32)
        for h, part in enumerate(normed_heads(raw + bias[1:2, :], gain[1:2, :])):
            store(part, slice(h * HD, (h + 1) * HD))

    @pl.when(step == 1)
    def _():
        raw = jnp.dot(rows[...], weight[0], preferred_element_type=jnp.float32)
        store((raw + bias[2:3, :]).astype(jnp.bfloat16), slice(LW, 2 * LW))


def join_rows(dst, parts):
    for i, part in enumerate(parts):
        dst[i * ROWS : (i + 1) * ROWS, :] = part[...]


def kv_half_kernel(m1, m3, m2, weight, bias, gain, out, rows):
    step = pl.program_id(0)

    @pl.when(step == 0)
    def _():
        join_rows(rows, (m1, m3, m2))

    def store(part, cols):
        out[:, cols] = part

    kv_both(step, rows, weight, bias, gain, store)


def kv_rest_kernel(m1, m3, m2, weight, bias, gain, half, ra, la, kv_b, right, left, rows):
    step = pl.program_id(0)

    def place(values, at, cols):
        kv_b[at : at + ROWS, cols] = values[0:ROWS]
        kv_b[TILE + at : TILE + at + ROWS, cols] = values[ROWS : 2 * ROWS]
        for out in (right, left):
            out[TILE + at : TILE + at + ROWS, cols] = values[2 * ROWS :]

    @pl.when(step == 0)
    def _():
        join_rows(rows, (m1, m3, m2))
        right[0:TILE, :] = ra[...]
        left[0:TILE, :] = la[...]
        place(half[...], 0, slice(0, 2 * LW))

    kv_both(step, rows, weight, bias, gain, lambda part, cols: place(part, ROWS, cols))


def project_others(kernel, mod, weight, bias, gain, more, out_rows):
    whole = lambda shape: pl.BlockSpec(shape, lambda c: (0,) * len(shape))
    return pl.pallas_call(
        kernel,
        grid=(2,),
        in_specs=[whole((ROWS, D))] * 3
        + [pl.BlockSpec((1, D, LW), lambda c: (1 + c, 0, 0)), whole((3, LW)), whole((2, HD))]
        + [whole((n, 2 * LW)) for n, _ in more],
        out_specs=[whole((n, 2 * LW)) for n in out_rows],
        out_shape=[jax.ShapeDtypeStruct((n, 2 * LW), jnp.bfloat16) for n in out_rows],
        scratch_shapes=[pltpu.VMEM((3 * ROWS, D), jnp.bfloat16)],
        compiler_params=pltpu.CompilerParams(vmem_limit_bytes=BIG * MIB),
        cost_estimate=COST,
        name="project_others",
    )(*mod, weight, bias, gain, *(array for _, array in more))


def q_kernel(parts, *refs):
    weight, bias, gain, q_ref, mod_ref = refs[parts:]
    for i in range(parts):
        mod_ref[i * ROWS : (i + 1) * ROWS, :] = refs[i][...]
    raw = jnp.dot(mod_ref[...], weight[0], preferred_element_type=jnp.float32)
    for h, part in enumerate(normed_heads(raw + bias[0:1, :], gain[0:1, :])):
        q_ref[:, h * HD : (h + 1) * HD] = part


def project(kernel, first, count, mod, weight, bias, gain, carry=(), tiles=None):
    parts = len(mod)
    rows = parts * ROWS
    out_rows = [rows - TILE] + [2 * TILE] * len(carry) if carry else [rows + (NOTE if tiles is not None else 0)]
    noted = [tiles] if tiles is not None else []
    whole = lambda shape: pl.BlockSpec(shape, lambda c: (0,) * len(shape))
    out = pl.pallas_call(
        kernel,
        grid=(count,),
        in_specs=[whole((ROWS, D))] * parts
        + [pl.BlockSpec((1, D, LW), lambda c: (first + c, 0, 0)), whole((3, LW)), whole((2, HD))]
        + [whole((TILE, 2 * LW))] * len(carry)
        + [SMEM()] * len(noted),
        out_specs=[whole((n, count * LW)) for n in out_rows],
        out_shape=[jax.ShapeDtypeStruct((n, count * LW), jnp.bfloat16) for n in out_rows],
        scratch_shapes=[pltpu.VMEM((rows, D), jnp.bfloat16)],
        compiler_params=pltpu.CompilerParams(vmem_limit_bytes=BIG * MIB),
        cost_estimate=COST,
        name="project",
    )(*mod, weight, bias, gain, *carry, *noted)
    return out if carry else out[0]


def project_kv(mod, *args, carry=(), tiles=None):
    return project(functools.partial(kv_kernel, len(mod), len(carry)), 1, 2, mod, *args, carry=carry, tiles=tiles)


def project_q(mod, *args):
    return project(functools.partial(q_kernel, len(mod)), 0, 1, mod, *args)


def pick_tile(dst, row, chunks, place):
    a, b, c = chunks

    @pl.when(place == 0)
    def _():
        dst[row : row + TILE, :] = a[...]

    @pl.when(jnp.logical_or(place == 1, place == 2))
    def _():
        dst[row : row + TILE, :] = b[pl.ds(pl.multiple_of((place - 1) * TILE, TILE), TILE), :]

    @pl.when(place == 3)
    def _():
        dst[row : row + TILE, :] = c[...]


def place_of(tile, head):
    step = ((tile & 3) - (head >> 1)) & 3
    return step ^ (step >> 1)


def select_kernel(head, want_left, want_right, la, lb, lc, ra, rb, rc, left, right):
    for k in range(2):
        pick_tile(left, k * TILE, (la, lb, lc), place_of(want_left[0, 12 + k], head[0]))
        pick_tile(right, k * TILE, (ra, rb, rc), place_of(want_right[0, 14 + k], head[0]))


def select_tiles(head, want_left, want_right, left, right):
    return pl.pallas_call(
        select_kernel,
        grid=(1,),
        in_specs=[SMEM()] * 3 + chunk_specs((0, 0)) * 2,
        out_specs=[whole_spec((2 * TILE, 2 * LW))] * 2,
        out_shape=[jax.ShapeDtypeStruct((2 * TILE, 2 * LW), jnp.bfloat16)] * 2,
        compiler_params=pltpu.CompilerParams(vmem_limit_bytes=BIG * MIB),
        cost_estimate=COST,
        name="select_tiles",
    )(head, want_left, want_right, *left, *right)


def accumulate(kv, q_block, live, num, den, first):
    scale = HD**-0.5 * math.log2(math.e)
    for h in range(HEADS):
        cols = slice(h * HD, (h + 1) * HD)
        scores = lax.dot_general(
            q_block(cols), kv[:, cols], (((1,), (1,)), ((), ())), preferred_element_type=jnp.float32
        )
        weights = jnp.exp2(scores * scale)
        parts = []
        for t in range(weights.shape[1] // TILE):
            w = weights[:, t * TILE : (t + 1) * TILE]
            if live is not None:
                w = jnp.where(live(t), w, 0.0)
            parts.append(w)
        total = functools.reduce(jnp.add, parts)
        rounded = jnp.concatenate([w.astype(jnp.bfloat16) for w in parts], axis=1)
        mixed = jnp.dot(rounded, kv[:, LW + h * HD : LW + (h + 1) * HD], preferred_element_type=jnp.float32)
        if first:
            num[0][:, cols] = mixed
            den[0][:, cols] = total
        else:
            num[0][:, cols] = num[1][:, cols] + mixed
            den[0][:, cols] = den[1][:, cols] + total


QB = 256


def own_kernel(q, a, b, c, num, den, kbuf):
    @pl.when(pl.program_id(0) == 0)
    def _():
        kbuf[0:TILE, :] = a[...]
        kbuf[TILE : 3 * TILE, :] = b[...]
        kbuf[3 * TILE :, :] = c[...]

    accumulate(kbuf, lambda cols: q[:, cols], None, (num,), (den,), True)


def hop_kernel(base, head, tiles, count, q, la, lb, lc, ra, rb, rc, num_in, den_in, num, den, kbuf):
    @pl.when(pl.program_id(0) == 0)
    def _():
        for k in range(2):
            pick_tile(kbuf, k * TILE, (la, lb, lc), place_of(tiles[0, base + k], head[0]))
            pick_tile(kbuf, (2 + k) * TILE, (ra, rb, rc), place_of(tiles[0, base + 2 + k], head[0]))

    live = lambda t: base + t < count[0]
    accumulate(kbuf, lambda cols: q[:, cols], live, (num, num_in), (den, den_in), False)


def rows_spec(width):
    return pl.BlockSpec((QB, width), lambda i: (i, 0))


def whole_spec(shape):
    return pl.BlockSpec(shape, lambda i: (0,) * len(shape))


ACC = [jax.ShapeDtypeStruct((512, LW), jnp.float32)] * 2
KBUF = [pltpu.VMEM((4 * TILE, 2 * LW), jnp.bfloat16)]


def chunk_specs(halves):
    a, c = halves
    return [
        pl.BlockSpec((TILE, 2 * LW), lambda i: (a, 0)),
        pl.BlockSpec((2 * TILE, 2 * LW), lambda i: (0, 0)),
        pl.BlockSpec((TILE, 2 * LW), lambda i: (c, 0)),
    ]


def attend_own(q, chunks):
    return pl.pallas_call(
        own_kernel,
        grid=(512 // QB,),
        in_specs=[rows_spec(LW)] + chunk_specs((0, 1)),
        out_specs=[rows_spec(LW)] * 2,
        out_shape=ACC,
        scratch_shapes=KBUF,
        compiler_params=pltpu.CompilerParams(vmem_limit_bytes=BIG * MIB),
        cost_estimate=COST,
        name="attend_own",
    )(q, *chunks)


def attend_hop(hop, halves, head, tiles, count, q, left, right, num, den):
    return pl.pallas_call(
        functools.partial(hop_kernel, 4 * (hop - 1)),
        grid=(512 // QB,),
        in_specs=[SMEM()] * 3 + [rows_spec(LW)] + chunk_specs(halves) * 2 + [rows_spec(LW)] * 2,
        out_specs=[rows_spec(LW)] * 2,
        out_shape=ACC,
        scratch_shapes=KBUF,
        compiler_params=pltpu.CompilerParams(vmem_limit_bytes=BIG * MIB),
        cost_estimate=COST,
        name="attend_hop",
    )(head, tiles, count, q, *left, *right, num, den)


def last_kernel(base, head, count, q, left, right, num_in, den_in, own, sib, edge_a, edge_b, kbuf, num, den):
    step = pl.program_id(0)

    @pl.when(step == 0)
    def _():
        kbuf[0 : 2 * TILE, :] = left[...]
        kbuf[2 * TILE :, :] = right[...]

    live = lambda t: base + t < count[0]
    accumulate(kbuf, lambda cols: q[:, cols], live, (num, num_in), (den, den_in), False)
    for h in range(HEADS):
        cols = slice(h * HD, (h + 1) * HD)
        total = jnp.sum(den[:, cols], axis=-1, keepdims=True)
        out = (num[:, cols] / total).astype(jnp.bfloat16)
        for t in range(QB // TILE):
            at = pl.ds(pl.multiple_of(step * (QB // 2) + t * ROWS, ROWS), ROWS)
            own[at, cols] = out[t * TILE : t * TILE + ROWS]
            sib[at, cols] = out[t * TILE + ROWS : (t + 1) * TILE]

    @pl.when(step == 512 // QB - 1)
    def _():
        core = head[0] & 1
        edge_a[...] = sib[pl.ds(pl.multiple_of(place_of(3 * (1 - core), head[0]) * ROWS, ROWS), ROWS), :]
        edge_b[...] = own[pl.ds(pl.multiple_of(place_of(3 * core, head[0]) * ROWS, ROWS), ROWS), :]


def attend_last(head, count, q, left, right, num, den):
    half = jax.ShapeDtypeStruct((256, LW), jnp.bfloat16)
    edge = jax.ShapeDtypeStruct((ROWS, LW), jnp.bfloat16)
    return pl.pallas_call(
        functools.partial(last_kernel, 12),
        grid=(512 // QB,),
        in_specs=[SMEM()] * 2
        + [rows_spec(LW)]
        + [whole_spec((2 * TILE, 2 * LW))] * 2
        + [rows_spec(LW)] * 2,
        out_specs=[whole_spec((256, LW))] * 2 + [whole_spec((ROWS, LW))] * 2,
        out_shape=[half, half, edge, edge],
        scratch_shapes=KBUF + [pltpu.VMEM((QB, LW), jnp.float32)] * 2,
        compiler_params=pltpu.CompilerParams(vmem_limit_bytes=BIG * MIB),
        cost_estimate=COST,
        name="attend_last",
    )(head, count, q, left, right, num, den)


NCOL = 768


def strip_of(head, window, strips):
    core = head[0] & 1
    return place_of(3 * core, head[0]), strips[(window[0] + core + WINDOWS - 1) & (WINDOWS - 1)], 1 - core


def halve_shared(a, rows, place, shared, top):
    a[...] = rows[...]
    row = lax.broadcasted_iota(jnp.int32, (ROWS, 1), 0)
    low = jnp.where(top == 1, 0, OV - shared)
    keep = jnp.where(jnp.logical_and(row >= low, row < low + shared), 0.5, 1.0)
    at = pl.ds(pl.multiple_of(place * ROWS, ROWS), ROWS)
    a[at, :] = (rows[at, :].astype(jnp.float32) * keep).astype(jnp.bfloat16)


dot = functools.partial(jnp.dot, preferred_element_type=jnp.float32)


def out_own_kernel(head, window, strips, own, w_own, part, a_own):
    @pl.when(pl.program_id(0) == 0)
    def _():
        halve_shared(a_own, own, *strip_of(head, window, strips))

    part[...] = dot(a_own[...], w_own[...])


def out_kernel(head, window, strips, part, sib, edge_own, edge_sib, w_own, w_sib, o0, o1, o3, o2, a_sib, e_own, e_sib):
    place, shared, top = strip_of(head, window, strips)

    @pl.when(pl.program_id(0) == 0)
    def _():
        halve_shared(a_sib, sib, place, shared, top)
        i = lax.broadcasted_iota(jnp.int32, (ROWS, ROWS), 0)
        j = lax.broadcasted_iota(jnp.int32, (ROWS, ROWS), 1)
        offset = jnp.where(top == 1, OV - shared, shared - OV)
        shift = jnp.where(j == i + offset, 0.5, 0.0).astype(jnp.bfloat16)
        e_own[...] = dot(shift, edge_own[...]).astype(jnp.bfloat16)
        e_sib[...] = dot(shift, edge_sib[...]).astype(jnp.bfloat16)

    main = part[...] + dot(a_sib[...], w_sib[...])
    extra = dot(e_own[...], w_own[...]) + dot(e_sib[...], w_sib[...])
    for k, ref in enumerate((o0, o1, o3, o2)):
        block = main[k * ROWS : (k + 1) * ROWS]
        ref[...] = (block + jnp.where(place == k, extra, 0.0)).astype(ref.dtype)


def out_cols(rows):
    return pl.BlockSpec((rows, NCOL), lambda i: (0, i))


def out_own(head, window, strips, own, w_own):
    return pl.pallas_call(
        out_own_kernel,
        grid=(D // NCOL,),
        in_specs=[SMEM()] * 3 + [whole_spec((256, LW)), out_cols(LW)],
        out_specs=out_cols(256),
        out_shape=jax.ShapeDtypeStruct((256, D), jnp.float32),
        scratch_shapes=[pltpu.VMEM((256, LW), jnp.bfloat16)],
        compiler_params=pltpu.CompilerParams(vmem_limit_bytes=BIG * MIB),
        cost_estimate=COST,
        name="out_own",
    )(head, window, strips, own, w_own)


def out_project(head, window, strips, part, sib, edge_own, edge_sib, w_own, w_sib):
    sent = jax.ShapeDtypeStruct((ROWS, D), jnp.bfloat16)
    return pl.pallas_call(
        out_kernel,
        grid=(D // NCOL,),
        in_specs=[SMEM()] * 3
        + [out_cols(256), whole_spec((256, LW))]
        + [whole_spec((ROWS, LW))] * 2
        + [out_cols(LW)] * 2,
        out_specs=[out_cols(ROWS)] * 4,
        out_shape=[jax.ShapeDtypeStruct((ROWS, D), jnp.float32), sent, sent, sent],
        scratch_shapes=[pltpu.VMEM((256, LW), jnp.bfloat16)] + [pltpu.VMEM((ROWS, LW), jnp.bfloat16)] * 2,
        compiler_params=pltpu.CompilerParams(vmem_limit_bytes=BIG * MIB),
        cost_estimate=COST,
        name="out_project",
    )(head, window, strips, part, sib, edge_own, edge_sib, w_own, w_sib)


def shards(
    latents,
    modulation,
    qkv_weight,
    qkv_bias,
    norm_gain,
    out_weight,
    out_bias,
    key_tiles,
    key_count,
    strip_rows,
):
    head = lax.axis_index("head").reshape(1)
    window = lax.axis_index("win").reshape(1)
    weight = jnp.transpose(qkv_weight, (1, 0, 2))
    args = (weight, qkv_bias, norm_gain)
    barrier = lax.optimization_barrier

    mod0 = modulate(latents, modulation)
    sib0 = swap_core(mod0)
    mod1, mod3 = to_y(mod0, -1), to_y(mod0, 1)
    mod2 = to_y(mod0, 2)
    kv_a = project_kv([mod0, sib0], *args, tiles=key_tiles)
    ra1, la1 = along_win(kv_a, 1), along_win(kv_a, -1)
    mod1, mod3, mod2, ra1, la1 = barrier((mod1, mod3, mod2, ra1, la1))
    sib1, sib3, sib2 = swap_core(mod1), swap_core(mod3), swap_core(mod2)
    (half,) = project_others(kv_half_kernel, (mod1, mod3, mod2), *args, (), (3 * ROWS,))
    half, sib1, sib3, sib2 = barrier((half, sib1, sib3, sib2))
    more = ((3 * ROWS, half), (TILE, ra1), (TILE, la1))
    kv_b, right_ac, left_ac = project_others(kv_rest_kernel, (sib1, sib3, sib2), *args, more, (2 * TILE,) * 3)
    rb1, lb1 = along_win(kv_b, 1), along_win(kv_b, -1)
    rac2, lac2 = along_win(right_ac, 1), along_win(left_ac, -1)
    kv_b, w_sent = barrier((kv_b, out_weight))
    w_sib = swap_core(w_sent)
    q = project_q([mod0, sib0, mod1, sib1, mod3, sib3, mod2, sib2], *args)
    hop_args = (head, key_tiles, key_count, q)
    num, den = attend_own(q, (kv_a, kv_b, right_ac))
    rac2, lac2, num, den, w_sib = barrier((rac2, lac2, num, den, w_sib))
    rb2, lb2 = along_win(rb1, 1), along_win(lb1, -1)
    rac3, lac3 = along_win(rac2, 1), along_win(lac2, -1)
    num, den = attend_hop(1, (0, 1), *hop_args, (la1, lb1, lac2), (ra1, rb1, rac2), num, den)
    rb2, lb2, num, den = barrier((rb2, lb2, num, den))
    rb3, lb3 = along_win(rb2, 1), along_win(lb2, -1)
    rc3, lc3 = along_win(rac3[TILE:], 1), along_win(lac3[TILE:], -1)
    num, den = attend_hop(2, (0, 1), *hop_args, (lac2, lb2, lac3), (rac2, rb2, rac3), num, den)
    rb3, lb3, rc3, lc3, num, den = barrier((rb3, lb3, rc3, lc3, num, den))
    right, left = (rac3, rb3, rc3), (lac3, lb3, lc3)
    tiles_prev, tiles_next = (x[TILE : TILE + 1, : 2 * NB].astype(jnp.int32) for x in (ra1, la1))
    last_left, last_right = select_tiles(head, tiles_prev, tiles_next, left, right)
    last_left, last_right = along_win(last_left, -1), along_win(last_right, 1)
    num, den = attend_hop(3, (0, 0), *hop_args, right=right, left=left, num=num, den=den)

    own, sib, edge_a, edge_b = attend_last(head, key_count, q, last_left, last_right, num, den)
    edge_own = lax.ppermute(edge_a, ("win", "head"), strip_pairs(0))
    edge_sib = lax.ppermute(edge_b, ("win", "head"), strip_pairs(1))
    sib = swap_core(sib)
    part = out_own(head, window, strip_rows, own, out_weight)
    part, edge_own, edge_sib, sib = barrier((part, edge_own, edge_sib, sib))
    o0, o1, o3, o2 = out_project(head, window, strip_rows, part, sib, edge_own, edge_sib, out_weight, w_sib)
    total = o0
    for part in (to_y(o1, 1), to_y(o3, -1), to_y(o2, 2)):
        total = total + part.astype(jnp.float32)
    result = latents.astype(jnp.float32) + modulation[2] * (total + out_bias)
    return result.astype(jnp.bfloat16)


def solution(mesh):
    in_specs = (
        P(("win", "head"), None),
        P(),
        P(None, None, "head"),
        P(None, "head"),
        P(),
        P("head", None),
        P(),
        P("win", None),
        P("win"),
        P(),
    )
    out_specs = P(("win", "head"), None)
    return jax.shard_map(shards, mesh=mesh, in_specs=in_specs, out_specs=out_specs, check_vma=False)
```
